32 devices in a mesh: lat: 4 (over z), lon: 8 (over y, x, core).
Axes of the slice: x: 2, y: 2, z: 4, core: 2. Of those that a mesh axis runs over, the one named last changes fastest.
Arguments:
- winds: float32 [2, 256, 23040], P(None, 'lat', 'lon'), may hold values from -6 to 6
- thickness: float32 [256, 23040], P('lat', 'lon'), may hold values from 0.5 to 1.5
- tracer: float32 [256, 23040], P('lat', 'lon'), may hold values from -6 to 6
- cutoff: int32 [256], P('lat'), may hold values from 1 to 1440, as said below
- damping: float32 [256], P('lat'), may hold values from 0.2 to 1
Outputs:
- new_winds: float32 [2, 256, 23040], P(None, 'lat', 'lon')
- new_thickness: float32 [256, 23040], P('lat', 'lon')
- new_tracer: float32 [256, 23040], P('lat', 'lon')
The draws below stay inside these ranges and needn't reach their ends.
Inputs may be any that keep to these rules, and one draw needn't show every extreme that they name: cutoff is a wavenumber of 1 to 1440.
All inputs are finite; a program needn't handle non-finite values.
Results may differ from the reference program's by a relative error of at most 0.0003.
Values sent between devices are 32-bit elements; how exact they have to be, the bound alone decides.
A program may use at most 128 MiB of HBM per device.

```python
import jax
import jax.numpy as jnp
import numpy as np

NLON = 2880
LEV = 8
NLAT = 256


def draw_cutoff(key, part):
    half_count = NLON // 2
    row_step = np.pi / NLAT
    latitude = -np.pi / 2 + (np.arange(NLAT) + 0.5) * row_step
    edge_angle = np.pi / 4 + row_step / 2
    cap_rows = np.minimum(half_count, np.maximum(1, np.floor(half_count * np.cos(latitude) / np.cos(edge_angle) + 0.5)))
    row_index = np.arange(NLAT)
    edge_rows = (row_index == NLAT // 4 - 1) | (row_index == NLAT - NLAT // 4)
    keep_mask = jnp.asarray(np.where(edge_rows, 0, 1).astype(np.int32))
    cap_table = jnp.asarray(cap_rows.astype(np.int32))
    noise = jax.random.randint(key, (NLAT,), 0, 1 << 20, dtype=jnp.int32)
    return cap_table - noise % (cap_table // 2 + 1) * keep_mask


def block_levels(stream_key, dims, shards, least, top_value):
    def one(position, blocks):
        steps = jax.random.uniform(jax.random.fold_in(jax.random.fold_in(stream_key, 6), position), (blocks,), jnp.float32, least / len(shards), top_value / len(shards))
        return jnp.repeat(jnp.exp(steps), dims[position] // blocks).reshape((-1,) + (1,) * (len(dims) - position - 1))

    loudness = one(*shards[0])
    for cut in shards[1:]:
        loudness = loudness * one(*cut)
    return loudness


def bell_draw(rng, shape, scale, most, shards=(), kind=jnp.bfloat16):
    factor_of = block_levels(rng, shape, shards, -0.22, 0.18) if shards else 1.0
    array = jax.random.normal(rng, shape, jnp.float32) * scale * factor_of
    return jnp.minimum(jnp.maximum(array, -most), most).astype(kind)


def setup_inputs(seed: int = 0) -> dict:
    splits = jax.random.split(jax.random.key(seed), 6)
    winds = bell_draw(splits[0], (2, NLAT, NLON * LEV), 1.0, 6.0, ((1, 4), (2, 8)), jnp.float32)
    thickness = jnp.clip(0.5 + 1.0 * jax.random.uniform(splits[1], (NLAT, NLON * LEV), jnp.float32) ** block_levels(splits[1], (NLAT, NLON * LEV), ((0, 4), (1, 8)), -0.2, 0.2), 0.5, 1.5)
    tracer = bell_draw(splits[2], (NLAT, NLON * LEV), 1.0, 6.0, ((0, 4), (1, 8)), jnp.float32)
    cutoff = draw_cutoff(jax.random.fold_in(splits[5], 71), 0)
    damping = jnp.clip(0.2 + 0.8 * jax.random.uniform(splits[4], (NLAT,), jnp.float32) ** block_levels(splits[4], (NLAT,), ((0, 4),), -0.2, 0.2), 0.2, 1.0)
    return {"winds": winds, "thickness": thickness, "tracer": tracer, "cutoff": cutoff, "damping": damping}


def east_of(values):
    return jnp.roll(values, -1, axis=-1)


def west_of(values):
    return jnp.roll(values, 1, axis=-1)


def antipode(values):
    return jnp.roll(values, NLON // 2, axis=-1)


def stencil(zonal, meridional, layer, tracer_mass):
    lon_step = 2.0 * jnp.pi / NLON
    lat_step = jnp.pi / NLAT
    time_step = lon_step
    centers = -jnp.pi / 2 + (jnp.arange(NLAT, dtype=jnp.float32) + 0.5) * lat_step
    cos_center = jnp.cos(centers)[:, None]
    faces = jnp.arange(NLAT + 1, dtype=jnp.float32)
    cos_face = jnp.where((faces == 0) | (faces == NLAT), 0.0, jnp.cos(-jnp.pi / 2 + faces * lat_step))[:, None]
    zero_row = jnp.zeros((LEV, 1, NLON), jnp.float32)
    flux_east = 0.25 * (zonal + east_of(zonal)) * (layer + east_of(layer))
    tracer_east = 0.25 * (zonal + east_of(zonal)) * (tracer_mass + east_of(tracer_mass))
    padded_wind = jnp.concatenate([zero_row, meridional, zero_row], axis=1)
    padded_layer = jnp.concatenate([zero_row, layer, zero_row], axis=1)
    padded_tracer = jnp.concatenate([zero_row, tracer_mass, zero_row], axis=1)
    wind_face = padded_wind[:, :-1] + padded_wind[:, 1:]
    flux_north = 0.25 * wind_face * (padded_layer[:, :-1] + padded_layer[:, 1:]) * cos_face
    tracer_north = 0.25 * wind_face * (padded_tracer[:, :-1] + padded_tracer[:, 1:]) * cos_face
    layer_div = ((flux_east - west_of(flux_east)) / lon_step + (flux_north[:, 1:] - flux_north[:, :-1]) / lat_step) / cos_center
    tracer_div = ((tracer_east - west_of(tracer_east)) / lon_step + (tracer_north[:, 1:] - tracer_north[:, :-1]) / lat_step) / cos_center
    new_layer = layer - time_step * layer_div
    new_tracer = tracer_mass - time_step * tracer_div
    north_rows = jnp.concatenate([layer[:, 1:], antipode(layer[:, -1:])], axis=1)
    south_rows = jnp.concatenate([antipode(layer[:, :1]), layer[:, :-1]], axis=1)
    new_zonal = zonal - time_step * (east_of(layer) - west_of(layer)) / (2.0 * lon_step * cos_center)
    new_meridional = meridional - time_step * (north_rows - south_rows) / (2.0 * lat_step)
    return new_zonal, new_meridional, new_layer, new_tracer


def unfold(values):
    return jnp.transpose(values.reshape(NLAT, NLON, LEV), (2, 0, 1))


def fold(values):
    return jnp.transpose(values, (1, 2, 0)).reshape(NLAT, NLON * LEV)


def reference(winds, thickness, tracer, cutoff, damping):
    fields = jnp.stack([unfold(winds[0]), unfold(winds[1]), unfold(thickness), unfold(tracer)])
    wavenumber = jnp.arange(NLON // 2 + 1, dtype=jnp.float32)
    cut_float = cutoff.astype(jnp.float32)[:, None]
    ratios = cut_float / jnp.maximum(wavenumber, 1.0)[None, :]
    row_index = jnp.arange(NLAT, dtype=jnp.int32)
    is_polar = (row_index < NLAT // 4) | (row_index >= NLAT - NLAT // 4)
    factor = jnp.where((wavenumber[None, :] > cut_float) & is_polar[:, None], damping[:, None] * ratios * ratios, 1.0)
    spectrum = jnp.fft.rfft(fields, axis=-1)
    filtered = jnp.fft.irfft(spectrum * factor, n=NLON, axis=-1).astype(jnp.float32)
    new_zonal, new_meridional, new_layer, new_tracer = stencil(filtered[0], filtered[1], filtered[2], filtered[3])
    return jnp.stack([fold(new_zonal), fold(new_meridional)]), fold(new_layer), fold(new_tracer)
```

```python
import functools
import math

import jax
import jax.numpy as jnp
import numpy as np
from jax import lax
from jax.experimental import pallas as pl
from jax.experimental.pallas import tpu as pltpu
from jax.sharding import PartitionSpec as P

LEV = 8
LANES = 128
SUB = 8
MESH = pl.DeviceIdType.MESH
EXACT = lax.Precision.HIGHEST


def round_up(value, step):
    return -(-value // step) * step


def inner_length(columns):
    return max(a for a in range(1, LANES // LEV + 1) if columns % a == 0)


def dft_tables(length, inner):
    outer = length // inner
    half = outer // 2 + 1
    kept = round_up(half, SUB)
    p = np.arange(outer)
    k1 = np.arange(half)
    angle = 2.0 * np.pi * ((p[None, :] * k1[:, None]) % outer) / outer
    first = np.zeros((2 * kept, outer))
    first[:half] = np.cos(angle)
    first[kept : kept + half] = -np.sin(angle)
    twice = np.where((k1 == 0) | (2 * k1 == outer), 1.0, 2.0)[:, None] / length
    last = np.zeros((outer, 2 * kept))
    last[:, :half] = (twice * np.cos(angle)).T
    last[:, kept : kept + half] = (-twice * np.sin(angle)).T
    a = np.arange(inner)
    turn = 2.0 * np.pi * ((k1[:, None] * a[None, :]) % length) / length
    twiddle = np.zeros((2, kept, LANES))
    twiddle[0, :half, : inner * LEV] = np.repeat(np.cos(turn), LEV, axis=1)
    twiddle[1, :half, : inner * LEV] = np.repeat(-np.sin(turn), LEV, axis=1)
    small = 2.0 * np.pi * ((a[:, None] * a[None, :]) % inner) / inner
    eye = np.eye(LEV)

    def real_form(re, im):
        out = np.zeros((2 * LANES, 2 * LANES))
        used = inner * LEV
        out[:used, :used] = np.kron(re, eye)
        out[:used, LANES : LANES + used] = np.kron(im, eye)
        out[LANES : LANES + used, :used] = -np.kron(im, eye)
        out[LANES : LANES + used, LANES : LANES + used] = np.kron(re, eye)
        return out

    forward = real_form(np.cos(small), -np.sin(small))
    backward = real_form(np.cos(small), np.sin(small))
    k = k1[:, None] + outer * a[None, :]
    wave = np.zeros((kept, LANES))
    wave[:half, : inner * LEV] = np.repeat(np.minimum(k, length - k), LEV, axis=1)
    tables = (first, twiddle, forward, backward, last, wave)
    return [np.asarray(t, np.float32) for t in tables]


def plan(lat_size, lon_size, row_count):
    groups = row_count // SUB
    split = lon_size // groups
    planes = 1 if split == 4 else 2
    slots = 4 // (planes * split)
    return groups, split, planes, slots


def filter_kernel(
    lat_size,
    lon_size,
    inner,
    winds,
    thickness,
    tracer,
    params,
    first,
    twiddle,
    forward,
    backward,
    last,
    wave,
    filt,
    south,
    north,
    recv,
    spread,
    done,
    ret,
    own,
    ext,
    edge,
    edge_in,
    prm,
    fwd_send,
    fwd_recv,
    ret_send,
    ret_recv,
    halo_send,
    halo_recv,
    rim_send,
    own_sem,
    edge_send,
    edge_recv,
    prm_sem,
    filt_sem,
):
    row_count, width = thickness.shape
    padded = filt.shape[-1]
    groups, split, planes, slots = plan(lat_size, lon_size, row_count)
    used = inner * LEV
    pieces = width // used
    outer = pieces * lon_size
    kept = wave.shape[0]
    quarter = lat_size // 4
    bit = 1 << (lat_size.bit_length() - 3)
    polar_bands = [b for b in range(lat_size) if b < quarter or b >= lat_size - quarter]
    band = lax.axis_index("lat")
    lon = lax.axis_index("lon")
    is_polar = (band < quarter) | (band >= lat_size - quarter)
    lowbit = (band // bit) % 2
    partner = band + bit - 2 * bit * lowbit
    home = jnp.where(is_polar, band, partner)
    my_plane = jnp.where(is_polar, 0, 1)
    my_group = lax.rem(lon, groups)
    my_split = lon // groups

    def pair_of(b):
        return {b, b ^ bit} if planes == 2 else {b}

    linked = [[False] * lat_size for _ in range(lat_size)]
    for b in range(lat_size):
        linked[b][b] = True
    for pb in polar_bands:
        for worker in pair_of(pb):
            targets = pair_of(pb) | {t for t in (pb - 1, pb + 1) if 0 <= t < lat_size}
            for target in targets:
                linked[worker][target] = linked[target][worker] = True

    barrier = pltpu.get_barrier_semaphore()
    expected = jnp.int32(-1)
    for other in range(lat_size):
        who = [b for b in range(lat_size) if linked[b][other]]
        talks = functools.reduce(jnp.logical_or, [band == b for b in who])
        expected += jnp.where(talks, lon_size, 0)

        @pl.when(talks)
        def _():
            for step in range(lon_size):
                target = lax.rem(lon + step, lon_size)

                @pl.when((target != lon) | (band != other))
                def _():
                    pl.semaphore_signal(
                        barrier, inc=1, device_id={"lat": other, "lon": target}, device_id_type=MESH
                    )

        near = [b for b in range(lat_size) if abs(b - other) == 1 and not linked[b][other]]
        if near:
            beside = functools.reduce(jnp.logical_or, [band == b for b in near])
            expected += jnp.where(beside, 1, 0)

            @pl.when(beside)
            def _():
                pl.semaphore_signal(
                    barrier, inc=1, device_id={"lat": other, "lon": lon}, device_id_type=MESH
                )

    pl.semaphore_wait(barrier, expected)

    def copies(src, dst, ssem, rsem, lat_to, lon_to):
        remote = pltpu.make_async_remote_copy(
            src_ref=src,
            dst_ref=dst,
            send_sem=ssem,
            recv_sem=rsem,
            device_id={"lat": lat_to, "lon": lon_to},
            device_id_type=MESH,
        )
        local = pltpu.make_async_copy(src, dst, rsem)
        return remote, local

    def push(src, dst, ssem, rsem, lat_to, lon_to):
        remote, local = copies(src, dst, ssem, rsem, lat_to, lon_to)
        same = (lat_to == band) & (lon_to == lon)

        @pl.when(same)
        def _():
            local.start()

        @pl.when(jnp.logical_not(same))
        def _():
            remote.start()

    def sent(src, dst, ssem, rsem, lat_to, lon_to):
        remote, _ = copies(src, dst, ssem, rsem, lat_to, lon_to)
        same = (lat_to == band) & (lon_to == lon)

        @pl.when(jnp.logical_not(same))
        def _():
            remote.wait_send()

    def arrived(dst, rsem):
        pltpu.make_async_copy(dst, dst, rsem).wait()

    fields = [winds.at[0], winds.at[1], thickness, tracer]

    def forward_copies(action):
        for slot in range(slots):
            for step in range(groups):
                group = lax.rem(lon + step, groups)
                for part in range(split):
                    for plane in reversed(range(planes)):
                        target = part * groups + group
                        field = (plane * split + part) * slots + slot
                        rows = pl.ds(pl.multiple_of(group * SUB, SUB), SUB)
                        action(
                            fields[field].at[rows, :],
                            recv.at[slot, lon],
                            fwd_send.at[slot, plane, target],
                            fwd_recv.at[slot, lon],
                            partner if plane else band,
                            target,
                        )

    def param_copy():
        return pltpu.make_async_remote_copy(
            src_ref=params.at[my_group],
            dst_ref=prm,
            send_sem=prm_sem.at[0],
            recv_sem=prm_sem.at[1],
            device_id={"lat": partner, "lon": lon},
            device_id_type=MESH,
        )

    @pl.when(is_polar)
    def _():
        if planes == 2:
            param_copy().start()
        forward_copies(push)

    def edge_copy(side):
        shift = 1 if side else lon_size - 1
        return pltpu.make_async_remote_copy(
            src_ref=edge,
            dst_ref=edge_in.at[side],
            send_sem=edge_send.at[side],
            recv_sem=edge_recv.at[side],
            device_id={"lat": band, "lon": lax.rem(lon + shift, lon_size)},
            device_id_type=MESH,
        )

    def rim_copy(side, item):
        rows = pl.ds(0, SUB) if side == 0 else pl.ds(row_count - SUB, SUB)
        dst = north if side == 0 else south
        return pltpu.make_async_remote_copy(
            src_ref=ext.at[item + 1, rows, :],
            dst_ref=dst.at[item],
            send_sem=rim_send.at[side, item],
            recv_sem=halo_recv.at[1 - side, item],
            device_id={"lat": band - 1 if side == 0 else band + 1, "lon": lon},
            device_id_type=MESH,
        )

    def keep_copy():
        return pltpu.make_async_copy(ext, filt, filt_sem.at[0])

    @pl.when(jnp.logical_not(is_polar))
    def _():
        loads = [pltpu.make_async_copy(fields[f], own.at[f], own_sem.at[f]) for f in range(4)]
        for load in loads:
            load.start()
        for load in loads:
            load.wait()
        for item, f in enumerate((0, 2, 3)):
            edge[item, :, :LEV] = own[f, :, :LEV]
            edge[item, :, LEV : 2 * LEV] = own[f, :, width - LEV :]
        edge_copy(0).start()
        edge_copy(1).start()
        for f in range(4):
            ext[f, :, :width] = own[f]
        edge_copy(0).wait()
        edge_copy(1).wait()
        for item, f in enumerate((0, 2, 3)):
            ext[f, :, width : width + LEV] = edge_in[0, item, :, :LEV]
            ext[f, :, padded - LEV :] = edge_in[1, item, :, LEV : 2 * LEV]
        keep_copy().start()
        for side in range(2):
            for item in range(3):
                rim_copy(side, item).start()

    def return_copies(slot, action):
        field = (my_plane * split + my_split) * slots + slot
        rows = pl.ds(pl.multiple_of(my_group * SUB, SUB), SUB)
        for step in range(lon_size):
            target = lax.rem(lon + step, lon_size)
            action(
                ret.at[slot, target],
                filt.at[field, rows, :],
                ret_send.at[slot, target],
                ret_recv.at[slot, my_plane, lon],
                home,
                target,
            )
        item = jnp.maximum(field - 1, 0)
        opposite = lon_size // 2
        for side in range(2):
            at_edge = my_group == (0 if side == 0 else groups - 1)
            at_pole = home == (0 if side == 0 else lat_size - 1)
            lat_to = home - 1 if side == 0 else home + 1

            @pl.when(at_edge & (field >= 1) & jnp.logical_not(at_pole))
            def _():
                for target in range(lon_size):
                    action(
                        ret.at[slot, target],
                        (north if side == 0 else south).at[item],
                        halo_send.at[slot, side, target],
                        halo_recv.at[1 - side, item],
                        lat_to,
                        jnp.int32(target),
                    )

            @pl.when(at_edge & (field == 2) & at_pole)
            def _():
                for target in range(lon_size):
                    action(
                        ret.at[slot, target],
                        (south if side == 0 else north).at[1],
                        halo_send.at[slot, side, target],
                        halo_recv.at[side, 1],
                        home,
                        jnp.int32((target + opposite) % lon_size),
                    )

    batch = 4

    def work(slot):
        for s in range(lon_size):
            arrived(recv.at[slot, s], fwd_recv.at[slot, s])

        def spread_sector(s, carry):
            block = recv[slot, s]
            for p in range(pieces):
                piece = block[:, used * p : used * (p + 1)]
                if used < LANES:
                    blank = jnp.zeros((SUB, LANES - used), jnp.float32)
                    piece = jnp.concatenate([piece, blank], axis=1)
                spread[pl.ds(s * pieces + p, SUB, stride=outer), :] = piece
            return carry

        lax.fori_loop(0, lon_size, spread_sector, 0)

        def some_rows(step, carry):
            base = step * batch
            rows = [spread[pl.ds((base + j) * outer, outer), :] for j in range(batch)]
            x = jnp.concatenate(rows, axis=1)
            y = jnp.dot(first[...], x, precision=EXACT, preferred_element_type=jnp.float32)
            tr, ti = twiddle[0], twiddle[1]
            z = []
            for j in range(batch):
                yr = y[:kept, j * LANES : (j + 1) * LANES]
                yi = y[kept:, j * LANES : (j + 1) * LANES]
                z.append(jnp.concatenate([yr * tr - yi * ti, yr * ti + yi * tr], axis=1))
            z = jnp.concatenate(z, axis=0)
            spectrum = jnp.dot(z, forward[...], precision=EXACT, preferred_element_type=jnp.float32)
            k = wave[...]
            inverse_k = 1.0 / jnp.maximum(k, 1.0)
            weighted = []
            for j in range(batch):
                cut = prm[pl.ds(base + j, 1), :]
                damp = prm[pl.ds(SUB + base + j, 1), :]
                ratio = cut * inverse_k
                factor = jnp.where(k > cut, damp * ratio * ratio, 1.0)
                weighted.append(
                    spectrum[j * kept : (j + 1) * kept] * jnp.concatenate([factor, factor], axis=1)
                )
            weighted = jnp.concatenate(weighted, axis=0)
            v = jnp.dot(weighted, backward[...], precision=EXACT, preferred_element_type=jnp.float32)
            u = []
            for j in range(batch):
                vr = v[j * kept : (j + 1) * kept, :LANES]
                vi = v[j * kept : (j + 1) * kept, LANES:]
                u.append(jnp.concatenate([vr * tr + vi * ti, vi * tr - vr * ti], axis=0))
            u = jnp.concatenate(u, axis=1)
            out = jnp.dot(last[...], u, precision=EXACT, preferred_element_type=jnp.float32)
            for j in range(batch):
                done[pl.ds((base + j) * outer, outer), :] = out[:, j * LANES : (j + 1) * LANES]
            return carry

        lax.fori_loop(0, SUB // batch, some_rows, 0)

        def gather_sector(s, carry):
            for p in range(pieces):
                piece = done[pl.ds(s * pieces + p, SUB, stride=outer), :]
                ret[slot, s, :, used * p : used * (p + 1)] = piece[:, :used]
            east = lax.rem(s + 1, lon_size) * pieces
            west = lax.rem(s + lon_size - 1, lon_size) * pieces + pieces - 1
            ret[slot, s, :, width : width + LEV] = done[pl.ds(east, SUB, stride=outer), :][:, :LEV]
            ret[slot, s, :, padded - LEV :] = done[pl.ds(west, SUB, stride=outer), :][
                :, used - LEV : used
            ]
            return carry

        lax.fori_loop(0, lon_size, gather_sector, 0)
        return_copies(slot, push)

    def all_work():
        for slot in range(slots):
            work(slot)
        for slot in range(slots):
            return_copies(slot, sent)

    @pl.when(is_polar)
    def _():
        prm[...] = params[my_group]

    if planes == 2:

        @pl.when(jnp.logical_not(is_polar))
        def _():
            param_copy().wait_recv()

        all_work()
    else:
        pl.when(is_polar)(all_work)

    @pl.when(is_polar)
    def _():
        if planes == 2:
            param_copy().wait_send()
        forward_copies(sent)
        for slot in range(slots):
            for plane in range(planes):
                for source in range(lon_size):
                    field = (plane * split + source // groups) * slots + slot
                    row = (source % groups) * SUB
                    arrived(
                        filt.at[field, pl.ds(row, SUB), :], ret_recv.at[slot, plane, source]
                    )

    @pl.when(jnp.logical_not(is_polar))
    def _():
        keep_copy().wait()
        for side in range(2):
            for item in range(3):
                rim_copy(side, item).wait_send()

    for side, rim in enumerate((south, north)):
        at_pole = band == (0 if side == 0 else lat_size - 1)
        arrived(rim.at[1], halo_recv.at[side, 1])

        @pl.when(jnp.logical_not(at_pole))
        def _():
            arrived(rim.at[0], halo_recv.at[side, 0])
            arrived(rim.at[2], halo_recv.at[side, 2])


def stencil_kernel(
    steps, lat_size, ratio, where_ref, here, below, above, south, north, coef, uv, new_h, new_q
):
    step = pl.program_id(0)
    band = where_ref[0]
    width = new_h.shape[-1]
    padded = here.shape[-1]
    first, final = step == 0, step == steps - 1
    low_pole = first & (band == 0)
    high_pole = final & (band == lat_size - 1)
    u, v, h, q = here[0], here[1], here[2], here[3]

    def south_of(x, item):
        row = jnp.where(first, south[item, SUB - 1 : SUB, :], below[item + 1, SUB - 1 : SUB, :])
        pole = south[1, 0:1, :] if item == 1 else jnp.zeros_like(row)
        row = jnp.where(low_pole, pole, row)
        return jnp.concatenate([row, x[: SUB - 1]], axis=0)

    def north_of(x, item):
        row = jnp.where(final, north[item, 0:1, :], above[item + 1, 0:1, :])
        pole = north[1, SUB - 1 : SUB, :] if item == 1 else jnp.zeros_like(row)
        row = jnp.where(high_pole, pole, row)
        return jnp.concatenate([x[1:], row], axis=0)

    def east_of(x):
        return pltpu.roll(x, padded - LEV, 1)

    def west_of(x):
        return pltpu.roll(x, LEV, 1)

    inv_c = coef[:, 0:1]
    face_s = coef[:, 1:2]
    face_n = coef[:, 2:3]
    he, hs, hn = east_of(h), south_of(h, 1), north_of(h, 1)
    hw = west_of(h)
    wind = 0.25 * (u + east_of(u))
    fx = wind * (h + he)
    gx = wind * (q + east_of(q))
    wind_s = face_s * (south_of(v, 0) + v)
    wind_n = face_n * (v + north_of(v, 0))
    fy = wind_n * (h + hn) - wind_s * (hs + h)
    gy = wind_n * (q + north_of(q, 2)) - wind_s * (south_of(q, 2) + q)
    out_h = h - ((fx - west_of(fx)) + fy) * inv_c
    out_q = q - ((gx - west_of(gx)) + gy) * inv_c
    out_u = u - (he - hw) * (0.5 * inv_c)
    out_v = v - (hn - hs) * (0.5 * ratio)
    uv[0] = out_u[:, :width]
    uv[1] = out_v[:, :width]
    new_h[...] = out_h[:, :width]
    new_q[...] = out_q[:, :width]


def per_device(winds, thickness, tracer, cutoff, damping):
    lat_size = lax.axis_size("lat")
    lon_size = lax.axis_size("lon")
    band = lax.axis_index("lat")
    row_count, width = thickness.shape
    columns = width // LEV
    length = columns * lon_size
    nlat = row_count * lat_size
    inner = inner_length(columns)
    outer = length // inner
    padded = round_up(width + 2 * LEV, LANES)
    groups, split, planes, slots = plan(lat_size, lon_size, row_count)
    params = jnp.stack([cutoff.astype(jnp.float32), damping]).reshape(2, groups, SUB)
    params = jnp.transpose(params, (1, 0, 2)).reshape(groups, 2 * SUB, 1)
    params = jnp.broadcast_to(params, (groups, 2 * SUB, LANES))
    tables = [jnp.asarray(t) for t in dft_tables(length, inner)]
    any_spec = pl.BlockSpec(memory_space=pl.ANY)
    vmem_spec = pl.BlockSpec(memory_space=pltpu.VMEM)
    f32 = jnp.float32
    filt, south, north = pl.pallas_call(
        functools.partial(filter_kernel, lat_size, lon_size, inner),
        out_shape=(
            jax.ShapeDtypeStruct((4, row_count, padded), f32),
            jax.ShapeDtypeStruct((3, SUB, padded), f32),
            jax.ShapeDtypeStruct((3, SUB, padded), f32),
        ),
        in_specs=[any_spec] * 3 + [vmem_spec] * (1 + len(tables)),
        out_specs=(any_spec,) * 3,
        scratch_shapes=[
            pltpu.VMEM((slots, lon_size, SUB, width), f32),
            pltpu.VMEM((SUB * outer, LANES), f32),
            pltpu.VMEM((SUB * outer, LANES), f32),
            pltpu.VMEM((slots, lon_size, SUB, padded), f32),
            pltpu.VMEM((4, row_count, width), f32),
            pltpu.VMEM((4, row_count, padded), f32),
            pltpu.VMEM((3, row_count, LANES), f32),
            pltpu.VMEM((2, 3, row_count, LANES), f32),
            pltpu.VMEM((2 * SUB, LANES), f32),
            pltpu.SemaphoreType.DMA((slots, planes, lon_size)),
            pltpu.SemaphoreType.DMA((slots, lon_size)),
            pltpu.SemaphoreType.DMA((slots, lon_size)),
            pltpu.SemaphoreType.DMA((slots, 2, lon_size)),
            pltpu.SemaphoreType.DMA((slots, 2, lon_size)),
            pltpu.SemaphoreType.DMA((2, 3)),
            pltpu.SemaphoreType.DMA((2, 3)),
            pltpu.SemaphoreType.DMA((4,)),
            pltpu.SemaphoreType.DMA((2,)),
            pltpu.SemaphoreType.DMA((2,)),
            pltpu.SemaphoreType.DMA((2,)),
            pltpu.SemaphoreType.DMA((1,)),
        ],
        compiler_params=pltpu.CompilerParams(
            collective_id=0, has_side_effects=True, vmem_limit_bytes=48 * 1024 * 1024
        ),
        cost_estimate=pl.CostEstimate(
            flops=4 * 10**9, bytes_accessed=4 * row_count * padded * 8, transcendentals=0
        ),
        name="polar_filter",
    )(winds, thickness, tracer, params, *tables)

    dlam = 2.0 * math.pi / length
    dphi = math.pi / nlat
    ratio = dlam / dphi
    rows = band * row_count + jnp.arange(row_count, dtype=jnp.int32)
    cos_center = jnp.cos(-math.pi / 2 + (rows.astype(f32) + 0.5) * dphi)

    def face(m):
        cosine = jnp.cos(-math.pi / 2 + m.astype(f32) * dphi)
        return jnp.where((m == 0) | (m == nlat), 0.0, cosine)

    coef = jnp.stack(
        [1.0 / cos_center, 0.25 * ratio * face(rows), 0.25 * ratio * face(rows + 1)], axis=1
    )
    steps = row_count // SUB
    where_am_i = band.astype(jnp.int32).reshape(1)
    block = (4, SUB, padded)
    whole = (3, SUB, padded)
    uv, new_h, new_q = pl.pallas_call(
        functools.partial(stencil_kernel, steps, lat_size, ratio),
        grid=(steps,),
        out_shape=(
            jax.ShapeDtypeStruct((2, row_count, width), f32),
            jax.ShapeDtypeStruct((row_count, width), f32),
            jax.ShapeDtypeStruct((row_count, width), f32),
        ),
        in_specs=[
            pl.BlockSpec(memory_space=pltpu.SMEM),
            pl.BlockSpec(block, lambda i: (0, i, 0)),
            pl.BlockSpec(block, lambda i: (0, jnp.maximum(i - 1, 0), 0)),
            pl.BlockSpec(block, lambda i: (0, jnp.minimum(i + 1, steps - 1), 0)),
            pl.BlockSpec(whole, lambda i: (0, 0, 0)),
            pl.BlockSpec(whole, lambda i: (0, 0, 0)),
            pl.BlockSpec((SUB, 3), lambda i: (i, 0)),
        ],
        out_specs=(
            pl.BlockSpec((2, SUB, width), lambda i: (0, i, 0)),
            pl.BlockSpec((SUB, width), lambda i: (i, 0)),
            pl.BlockSpec((SUB, width), lambda i: (i, 0)),
        ),
        compiler_params=pltpu.CompilerParams(vmem_limit_bytes=32 * 1024 * 1024),
        name="stencil",
    )(where_am_i, filt, filt, filt, south, north, coef)
    return uv, new_h, new_q


def solution(mesh):
    placed = (P(None, "lat", "lon"), P("lat", "lon"), P("lat", "lon"), P("lat"), P("lat"))
    return jax.shard_map(
        per_device,
        mesh=mesh,
        in_specs=placed,
        out_specs=(P(None, "lat", "lon"), P("lat", "lon"), P("lat", "lon")),
        check_vma=False,
    )
```

```python
import functools
import math

import jax
import jax.numpy as jnp
import numpy as np
from jax import lax
from jax.experimental import pallas as pl
from jax.experimental.pallas import tpu as pltpu
from jax.sharding import PartitionSpec as P

LEV = 8
LANES = 128
SUB = 8
MESH = pl.DeviceIdType.MESH
TABLES = 7
EXACT = lax.Precision.HIGHEST


def round_up(value, step):
    return -(-value // step) * step


def inner_length(columns):
    return max(a for a in range(1, LANES // LEV + 1) if columns % a == 0)


def halves(x):
    high = x.astype(jnp.bfloat16)
    return high, (x - high.astype(jnp.float32)).astype(jnp.bfloat16)


def left_dot(parts, x):
    high, low = halves(x)
    stacked = jnp.concatenate([high, low, high], axis=0)
    return jnp.dot(parts[...], stacked, preferred_element_type=jnp.float32)


def right_dot(x, parts):
    high, low = halves(x)
    stacked = jnp.concatenate([high, low, high], axis=1)
    return jnp.dot(stacked, parts[...], preferred_element_type=jnp.float32)


def dft_tables(length, inner):
    outer = length // inner
    half = outer // 2 + 1
    kept = round_up(half, SUB)
    p = np.arange(outer)
    k1 = np.arange(half)
    angle = 2.0 * np.pi * ((p[None, :] * k1[:, None]) % outer) / outer
    first = np.zeros((2 * kept, outer))
    first[:half] = np.cos(angle)
    first[kept : kept + half] = -np.sin(angle)
    twice = np.where((k1 == 0) | (2 * k1 == outer), 1.0, 2.0)[:, None] / length
    last = np.zeros((outer, 2 * kept))
    last[:, :half] = (twice * np.cos(angle)).T
    last[:, kept : kept + half] = (-twice * np.sin(angle)).T
    a = np.arange(inner)
    turn = 2.0 * np.pi * ((k1[:, None] * a[None, :]) % length) / length
    twiddle = np.zeros((2, kept, LANES))
    twiddle[0, :half, : inner * LEV] = np.repeat(np.cos(turn), LEV, axis=1)
    twiddle[1, :half, : inner * LEV] = np.repeat(-np.sin(turn), LEV, axis=1)
    small = 2.0 * np.pi * ((a[:, None] * a[None, :]) % inner) / inner
    eye = np.eye(LEV)

    def real_form(re, im):
        out = np.zeros((2 * LANES, 2 * LANES))
        used = inner * LEV
        out[:used, :used] = np.kron(re, eye)
        out[:used, LANES : LANES + used] = np.kron(im, eye)
        out[LANES : LANES + used, :used] = -np.kron(im, eye)
        out[LANES : LANES + used, LANES : LANES + used] = np.kron(re, eye)
        return out

    forward = real_form(np.cos(small), -np.sin(small))
    backward = real_form(np.cos(small), np.sin(small))
    k = k1[:, None] + outer * a[None, :]
    wave = np.zeros((kept, LANES))
    wave[:half, : inner * LEV] = np.repeat(np.minimum(k, length - k), LEV, axis=1)
    average = np.zeros((LANES, LANES))
    average[: inner * LEV, : inner * LEV] = np.kron(np.ones((inner, inner)), eye) / length

    def left_parts(table):
        high, low = halves(np.asarray(table, np.float32))
        return np.concatenate([high, high, low], axis=1)

    def right_parts(table):
        high, low = halves(np.asarray(table, np.float32))
        return np.concatenate([high, high, low], axis=0)

    matrices = [left_parts(first), right_parts(forward), right_parts(backward), left_parts(last)]
    return matrices + [np.asarray(t, np.float32) for t in (twiddle, wave, average)]


def plan(lat_size, lon_size, row_count):
    groups = row_count // SUB
    split = lon_size // groups
    planes = 1 if split == 4 else 2
    slots = 4 // (planes * split)
    return groups, split, planes, slots


def filter_kernel(
    lat_size,
    lon_size,
    inner,
    winds,
    thickness,
    tracer,
    cutoff,
    damping,
    *rest,
):
    table_in, rest = rest[:TABLES], rest[TABLES:]
    (filt, south, north), rest = rest[:3], rest[3:]
    tables, rest = rest[:TABLES], rest[TABLES:]
    first, forward, backward, last, twiddle, wave, average = tables
    (

        recv,
    spread,
    done,
    ret,
    own,
    ext,
    edge,
    edge_in,
    prm,
    fwd_send,
    fwd_recv,
    ret_send,
    ret_recv,
    halo_send,
    halo_recv,
    rim_send,
    own_sem,
    edge_send,
    edge_recv,
    prm_sem,
    filt_sem,
    table_sem,
    ) = rest
    row_count, width = thickness.shape
    padded = filt.shape[-1]
    groups, split, planes, slots = plan(lat_size, lon_size, row_count)
    used = inner * LEV
    pieces = width // used
    outer = pieces * lon_size
    kept = wave.shape[0]
    quarter = lat_size // 4
    bit = 1 << (lat_size.bit_length() - 3)
    polar_bands = [b for b in range(lat_size) if b < quarter or b >= lat_size - quarter]
    band = lax.axis_index("lat")
    lon = lax.axis_index("lon")
    is_polar = (band < quarter) | (band >= lat_size - quarter)
    lowbit = (band // bit) % 2
    partner = band + bit - 2 * bit * lowbit
    home = jnp.where(is_polar, band, partner)
    my_plane = jnp.where(is_polar, 0, 1)
    my_group = lax.rem(lon, groups)
    my_split = lon // groups

    def pair_of(b):
        return {b, b ^ bit} if planes == 2 else {b}

    linked = [[False] * lat_size for _ in range(lat_size)]
    for b in range(lat_size):
        linked[b][b] = True
    for pb in polar_bands:
        for worker in pair_of(pb):
            targets = pair_of(pb) | {t for t in (pb - 1, pb + 1) if 0 <= t < lat_size}
            for target in targets:
                linked[worker][target] = linked[target][worker] = True

    table_loads = [
        pltpu.make_async_copy(table_in[i], tables[i], table_sem.at[i]) for i in range(TABLES)
    ]
    arrays = [winds.at[0], winds.at[1], thickness, tracer]
    loads = [pltpu.make_async_copy(arrays[f], own.at[f], own_sem.at[f]) for f in range(4)]
    for load in loads + table_loads:
        load.start()
    barrier = pltpu.get_barrier_semaphore()
    expected = jnp.int32(-1)
    for other in range(lat_size):
        who = [b for b in range(lat_size) if linked[b][other]]
        talks = functools.reduce(jnp.logical_or, [band == b for b in who])
        expected += jnp.where(talks, lon_size, 0)

        @pl.when(talks)
        def _():
            for step in range(lon_size):
                target = lax.rem(lon + step, lon_size)

                @pl.when((target != lon) | (band != other))
                def _():
                    pl.semaphore_signal(
                        barrier, inc=1, device_id={"lat": other, "lon": target}, device_id_type=MESH
                    )

        near = [b for b in range(lat_size) if abs(b - other) == 1 and not linked[b][other]]
        if near:
            beside = functools.reduce(jnp.logical_or, [band == b for b in near])
            expected += jnp.where(beside, 1, 0)

            @pl.when(beside)
            def _():
                pl.semaphore_signal(
                    barrier, inc=1, device_id={"lat": other, "lon": lon}, device_id_type=MESH
                )

    pl.semaphore_wait(barrier, expected)

    def copies(src, dst, ssem, rsem, lat_to, lon_to):
        remote = pltpu.make_async_remote_copy(
            src_ref=src,
            dst_ref=dst,
            send_sem=ssem,
            recv_sem=rsem,
            device_id={"lat": lat_to, "lon": lon_to},
            device_id_type=MESH,
        )
        local = pltpu.make_async_copy(src, dst, rsem)
        return remote, local

    def push(src, dst, ssem, rsem, lat_to, lon_to):
        remote, local = copies(src, dst, ssem, rsem, lat_to, lon_to)
        same = (lat_to == band) & (lon_to == lon)

        @pl.when(same)
        def _():
            local.start()

        @pl.when(jnp.logical_not(same))
        def _():
            remote.start()

    def sent(src, dst, ssem, rsem, lat_to, lon_to):
        remote, _ = copies(src, dst, ssem, rsem, lat_to, lon_to)
        same = (lat_to == band) & (lon_to == lon)

        @pl.when(jnp.logical_not(same))
        def _():
            remote.wait_send()

    def arrived(dst, rsem):
        pltpu.make_async_copy(dst, dst, rsem).wait()

    def forward_copies(slot, action):
        for step in range(groups):
            group = lax.rem(lon + step, groups)
            for part in range(split):
                for plane in reversed(range(planes)):
                    target = part * groups + group
                    field = (plane * split + part) * slots + slot
                    rows = pl.ds(pl.multiple_of(group * SUB, SUB), SUB)
                    action(
                        own.at[field, rows, :],
                        recv.at[slot, lon],
                        fwd_send.at[slot, plane, target],
                        fwd_recv.at[slot, lon],
                        partner if plane else band,
                        target,
                    )

    for load in loads:
        load.wait()

    def param_copy():
        return pltpu.make_async_remote_copy(
            src_ref=prm,
            dst_ref=prm,
            send_sem=prm_sem.at[0],
            recv_sem=prm_sem.at[1],
            device_id={"lat": partner, "lon": lon},
            device_id_type=MESH,
        )

    @pl.when(is_polar)
    def _():
        forward_copies(0, push)
        for j in range(SUB):
            row = my_group * SUB + j
            prm[j : j + 1, :] = jnp.full((1, LANES), cutoff[row].astype(jnp.float32))
            prm[SUB + j : SUB + j + 1, :] = jnp.full((1, LANES), damping[row])
        if planes == 2:
            param_copy().start()

    def edge_copy(side):
        shift = 1 if side else lon_size - 1
        return pltpu.make_async_remote_copy(
            src_ref=edge,
            dst_ref=edge_in.at[side],
            send_sem=edge_send.at[side],
            recv_sem=edge_recv.at[side],
            device_id={"lat": band, "lon": lax.rem(lon + shift, lon_size)},
            device_id_type=MESH,
        )

    def rim_copy(side, item):
        rows = pl.ds(0, SUB) if side == 0 else pl.ds(row_count - SUB, SUB)
        dst = north if side == 0 else south
        return pltpu.make_async_remote_copy(
            src_ref=ext.at[item + 1, rows, :],
            dst_ref=dst.at[item],
            send_sem=rim_send.at[side, item],
            recv_sem=halo_recv.at[1 - side, item],
            device_id={"lat": band - 1 if side == 0 else band + 1, "lon": lon},
            device_id_type=MESH,
        )

    def keep_copy():
        return pltpu.make_async_copy(ext, filt, filt_sem.at[0])

    @pl.when(jnp.logical_not(is_polar))
    def _():
        for item, f in enumerate((0, 2, 3)):
            edge[item, :, :LEV] = own[f, :, :LEV]
            edge[item, :, LEV : 2 * LEV] = own[f, :, width - LEV :]
        edge_copy(0).start()
        edge_copy(1).start()
        for f in range(4):
            ext[f, :, :width] = own[f]
        edge_copy(0).wait()
        edge_copy(1).wait()
        for item, f in enumerate((0, 2, 3)):
            ext[f, :, width : width + LEV] = edge_in[0, item, :, :LEV]
            ext[f, :, padded - LEV :] = edge_in[1, item, :, LEV : 2 * LEV]
        keep_copy().start()
        for side in range(2):
            for item in range(3):
                rim_copy(side, item).start()

    def return_copies(slot, action):
        field = (my_plane * split + my_split) * slots + slot
        rows = pl.ds(pl.multiple_of(my_group * SUB, SUB), SUB)
        for step in range(lon_size):
            target = lax.rem(lon + step, lon_size)
            action(
                ret.at[slot, target],
                filt.at[field, rows, :],
                ret_send.at[slot, target],
                ret_recv.at[slot, my_plane, lon],
                home,
                target,
            )
        item = jnp.maximum(field - 1, 0)
        opposite = lon_size // 2
        for side in range(2):
            at_edge = my_group == (0 if side == 0 else groups - 1)
            at_pole = home == (0 if side == 0 else lat_size - 1)
            lat_to = home - 1 if side == 0 else home + 1

            @pl.when(at_edge & (field >= 1) & jnp.logical_not(at_pole))
            def _():
                for target in range(lon_size):
                    action(
                        ret.at[slot, target],
                        (north if side == 0 else south).at[item],
                        halo_send.at[slot, side, target],
                        halo_recv.at[1 - side, item],
                        lat_to,
                        jnp.int32(target),
                    )

            @pl.when(at_edge & (field == 2) & at_pole)
            def _():
                for target in range(lon_size):
                    action(
                        ret.at[slot, target],
                        (south if side == 0 else north).at[1],
                        halo_send.at[slot, side, target],
                        halo_recv.at[side, 1],
                        home,
                        jnp.int32((target + opposite) % lon_size),
                    )

    batch = 4

    def work(slot):
        for s in range(lon_size):
            arrived(recv.at[slot, s], fwd_recv.at[slot, s])

        def spread_sector(s, carry):
            block = recv[slot, s]
            for p in range(pieces):
                piece = block[:, used * p : used * (p + 1)]
                if used < LANES:
                    blank = jnp.zeros((SUB, LANES - used), jnp.float32)
                    piece = jnp.concatenate([piece, blank], axis=1)
                spread[pl.ds(s * pieces + p, SUB, stride=outer), :] = piece
            return carry

        lax.fori_loop(0, lon_size, spread_sector, 0)

        def some_rows(step, carry):
            base = step * batch
            rows = [spread[pl.ds((base + j) * outer, outer), :] for j in range(batch)]
            sums = [jnp.sum(row, axis=0, keepdims=True) for row in rows] * (SUB // batch)
            mean = jnp.dot(
                jnp.concatenate(sums, axis=0),
                average[...],
                precision=EXACT,
                preferred_element_type=jnp.float32,
            )
            means = [mean[j : j + 1] for j in range(batch)]
            x = jnp.concatenate([rows[j] - means[j] for j in range(batch)], axis=1)
            y = left_dot(first, x)
            tr, ti = twiddle[0], twiddle[1]
            z = []
            for j in range(batch):
                yr = y[:kept, j * LANES : (j + 1) * LANES]
                yi = y[kept:, j * LANES : (j + 1) * LANES]
                z.append(jnp.concatenate([yr * tr - yi * ti, yr * ti + yi * tr], axis=1))
            z = jnp.concatenate(z, axis=0)
            spectrum = right_dot(z, forward)
            k = wave[...]
            inverse_k = 1.0 / jnp.maximum(k, 1.0)
            weighted = []
            for j in range(batch):
                cut = prm[pl.ds(base + j, 1), :]
                damp = prm[pl.ds(SUB + base + j, 1), :]
                ratio = cut * inverse_k
                factor = jnp.where(k > cut, damp * ratio * ratio, 1.0)
                weighted.append(
                    spectrum[j * kept : (j + 1) * kept] * jnp.concatenate([factor, factor], axis=1)
                )
            weighted = jnp.concatenate(weighted, axis=0)
            v = right_dot(weighted, backward)
            u = []
            for j in range(batch):
                vr = v[j * kept : (j + 1) * kept, :LANES]
                vi = v[j * kept : (j + 1) * kept, LANES:]
                u.append(jnp.concatenate([vr * tr + vi * ti, vi * tr - vr * ti], axis=0))
            u = jnp.concatenate(u, axis=1)
            out = left_dot(last, u)
            for j in range(batch):
                piece = out[:, j * LANES : (j + 1) * LANES] + means[j]
                done[pl.ds((base + j) * outer, outer), :] = piece
            return carry

        lax.fori_loop(0, SUB // batch, some_rows, 0)

        def gather_sector(s, carry):
            for p in range(pieces):
                piece = done[pl.ds(s * pieces + p, SUB, stride=outer), :]
                ret[slot, s, :, used * p : used * (p + 1)] = piece[:, :used]
            east = lax.rem(s + 1, lon_size) * pieces
            west = lax.rem(s + lon_size - 1, lon_size) * pieces + pieces - 1
            ret[slot, s, :, width : width + LEV] = done[pl.ds(east, SUB, stride=outer), :][:, :LEV]
            ret[slot, s, :, padded - LEV :] = done[pl.ds(west, SUB, stride=outer), :][
                :, used - LEV : used
            ]
            return carry

        lax.fori_loop(0, lon_size, gather_sector, 0)
        return_copies(slot, push)

    def all_work():
        for slot in range(slots):
            if slot + 1 < slots:

                @pl.when(is_polar)
                def _():
                    forward_copies(slot, sent)
                    forward_copies(slot + 1, push)

            work(slot)
        for slot in range(slots):
            return_copies(slot, sent)

    for load in table_loads:
        load.wait()

    if planes == 2:

        @pl.when(jnp.logical_not(is_polar))
        def _():
            param_copy().wait_recv()

        all_work()
    else:
        pl.when(is_polar)(all_work)

    @pl.when(is_polar)
    def _():
        if planes == 2:
            param_copy().wait_send()
        forward_copies(slots - 1, sent)
        for slot in range(slots):
            for plane in range(planes):
                for source in range(lon_size):
                    field = (plane * split + source // groups) * slots + slot
                    row = (source % groups) * SUB
                    arrived(
                        filt.at[field, pl.ds(row, SUB), :], ret_recv.at[slot, plane, source]
                    )

    @pl.when(jnp.logical_not(is_polar))
    def _():
        keep_copy().wait()
        for side in range(2):
            for item in range(3):
                rim_copy(side, item).wait_send()

    for side, rim in enumerate((south, north)):
        at_pole = band == (0 if side == 0 else lat_size - 1)
        arrived(rim.at[1], halo_recv.at[side, 1])

        @pl.when(jnp.logical_not(at_pole))
        def _():
            arrived(rim.at[0], halo_recv.at[side, 0])
            arrived(rim.at[2], halo_recv.at[side, 2])


def stencil_kernel(
    steps, lat_size, ratio, where_ref, here, below, above, south, north, coef, uv, new_h, new_q
):
    step = pl.program_id(0)
    band = where_ref[0]
    width = new_h.shape[-1]
    padded = here.shape[-1]
    first, final = step == 0, step == steps - 1
    low_pole = first & (band == 0)
    high_pole = final & (band == lat_size - 1)
    u, v, h, q = here[0], here[1], here[2], here[3]

    def south_of(x, item):
        row = jnp.where(first, south[item, SUB - 1 : SUB, :], below[item + 1, SUB - 1 : SUB, :])
        pole = south[1, 0:1, :] if item == 1 else jnp.zeros_like(row)
        row = jnp.where(low_pole, pole, row)
        return jnp.concatenate([row, x[: SUB - 1]], axis=0)

    def north_of(x, item):
        row = jnp.where(final, north[item, 0:1, :], above[item + 1, 0:1, :])
        pole = north[1, SUB - 1 : SUB, :] if item == 1 else jnp.zeros_like(row)
        row = jnp.where(high_pole, pole, row)
        return jnp.concatenate([x[1:], row], axis=0)

    def east_of(x):
        return pltpu.roll(x, padded - LEV, 1)

    def west_of(x):
        return pltpu.roll(x, LEV, 1)

    inv_c = coef[:, 0:1]
    face_s = coef[:, 1:2]
    face_n = coef[:, 2:3]
    he, hs, hn = east_of(h), south_of(h, 1), north_of(h, 1)
    hw = west_of(h)
    wind = 0.25 * (u + east_of(u))
    fx = wind * (h + he)
    gx = wind * (q + east_of(q))
    wind_s = face_s * (south_of(v, 0) + v)
    wind_n = face_n * (v + north_of(v, 0))
    fy = wind_n * (h + hn) - wind_s * (hs + h)
    gy = wind_n * (q + north_of(q, 2)) - wind_s * (south_of(q, 2) + q)
    out_h = h - ((fx - west_of(fx)) + fy) * inv_c
    out_q = q - ((gx - west_of(gx)) + gy) * inv_c
    out_u = u - (he - hw) * (0.5 * inv_c)
    out_v = v - (hn - hs) * (0.5 * ratio)
    uv[0] = out_u[:, :width]
    uv[1] = out_v[:, :width]
    new_h[...] = out_h[:, :width]
    new_q[...] = out_q[:, :width]


def per_device(winds, thickness, tracer, cutoff, damping):
    lat_size = lax.axis_size("lat")
    lon_size = lax.axis_size("lon")
    band = lax.axis_index("lat")
    row_count, width = thickness.shape
    columns = width // LEV
    length = columns * lon_size
    nlat = row_count * lat_size
    inner = inner_length(columns)
    outer = length // inner
    padded = round_up(width + 2 * LEV, LANES)
    groups, split, planes, slots = plan(lat_size, lon_size, row_count)
    tables = [jnp.asarray(t) for t in dft_tables(length, inner)]
    vmem_spec = pl.BlockSpec(memory_space=pltpu.VMEM)
    hbm_spec = pl.BlockSpec(memory_space=pltpu.HBM)
    smem_spec = pl.BlockSpec(memory_space=pltpu.SMEM)
    f32 = jnp.float32
    filt, south, north = pl.pallas_call(
        functools.partial(filter_kernel, lat_size, lon_size, inner),
        out_shape=(
            jax.ShapeDtypeStruct((4, row_count, padded), f32),
            jax.ShapeDtypeStruct((3, SUB, padded), f32),
            jax.ShapeDtypeStruct((3, SUB, padded), f32),
        ),
        in_specs=[hbm_spec] * 3 + [smem_spec] * 2 + [hbm_spec] * TABLES,
        out_specs=(vmem_spec,) * 3,
        scratch_shapes=[pltpu.VMEM(t.shape, t.dtype) for t in tables]
        + [
            pltpu.VMEM((slots, lon_size, SUB, width), f32),
            pltpu.VMEM((SUB * outer, LANES), f32),
            pltpu.VMEM((SUB * outer, LANES), f32),
            pltpu.VMEM((slots, lon_size, SUB, padded), f32),
            pltpu.VMEM((4, row_count, width), f32),
            pltpu.VMEM((4, row_count, padded), f32),
            pltpu.VMEM((3, row_count, LANES), f32),
            pltpu.VMEM((2, 3, row_count, LANES), f32),
            pltpu.VMEM((2 * SUB, LANES), f32),
            pltpu.SemaphoreType.DMA((slots, planes, lon_size)),
            pltpu.SemaphoreType.DMA((slots, lon_size)),
            pltpu.SemaphoreType.DMA((slots, lon_size)),
            pltpu.SemaphoreType.DMA((slots, 2, lon_size)),
            pltpu.SemaphoreType.DMA((slots, 2, lon_size)),
            pltpu.SemaphoreType.DMA((2, 3)),
            pltpu.SemaphoreType.DMA((2, 3)),
            pltpu.SemaphoreType.DMA((4,)),
            pltpu.SemaphoreType.DMA((2,)),
            pltpu.SemaphoreType.DMA((2,)),
            pltpu.SemaphoreType.DMA((2,)),
            pltpu.SemaphoreType.DMA((1,)),
            pltpu.SemaphoreType.DMA((TABLES,)),
        ],
        compiler_params=pltpu.CompilerParams(
            collective_id=0, has_side_effects=True, vmem_limit_bytes=54 * 1024 * 1024
        ),
        cost_estimate=pl.CostEstimate(
            flops=4 * 10**9, bytes_accessed=4 * row_count * padded * 8, transcendentals=0
        ),
        name="polar_filter",
    )(winds, thickness, tracer, cutoff, damping, *tables)

    dlam = 2.0 * math.pi / length
    dphi = math.pi / nlat
    ratio = dlam / dphi
    centers = np.cos(-np.pi / 2 + (np.arange(nlat) + 0.5) * dphi)
    faces = np.cos(-np.pi / 2 + np.arange(nlat + 1) * dphi)
    faces[0] = faces[-1] = 0.0
    faces = 0.25 * ratio * faces
    coef = jnp.asarray(np.stack([1.0 / centers, faces[:-1], faces[1:]], axis=1), f32)
    steps = row_count // SUB
    where_am_i = band.astype(jnp.int32).reshape(1)
    block = (4, SUB, padded)
    whole = (3, SUB, padded)
    uv, new_h, new_q = pl.pallas_call(
        functools.partial(stencil_kernel, steps, lat_size, ratio),
        grid_spec=pltpu.PrefetchScalarGridSpec(
            num_scalar_prefetch=1,
            grid=(steps,),
            in_specs=[
                pl.BlockSpec(block, lambda i, b: (0, i, 0)),
                pl.BlockSpec(block, lambda i, b: (0, jnp.maximum(i - 1, 0), 0)),
                pl.BlockSpec(block, lambda i, b: (0, jnp.minimum(i + 1, steps - 1), 0)),
                pl.BlockSpec(whole, lambda i, b: (0, 0, 0)),
                pl.BlockSpec(whole, lambda i, b: (0, 0, 0)),
                pl.BlockSpec((SUB, 3), lambda i, b: (b[0] * steps + i, 0)),
            ],
            out_specs=(
                pl.BlockSpec((2, SUB, width), lambda i, b: (0, i, 0)),
                pl.BlockSpec((SUB, width), lambda i, b: (i, 0)),
                pl.BlockSpec((SUB, width), lambda i, b: (i, 0)),
            ),
        ),
        out_shape=(
            jax.ShapeDtypeStruct((2, row_count, width), f32),
            jax.ShapeDtypeStruct((row_count, width), f32),
            jax.ShapeDtypeStruct((row_count, width), f32),
        ),
        compiler_params=pltpu.CompilerParams(vmem_limit_bytes=20 * 1024 * 1024),
        name="stencil",
    )(where_am_i, filt, filt, filt, south, north, coef)
    return uv, new_h, new_q


def solution(mesh):
    placed = (P(None, "lat", "lon"), P("lat", "lon"), P("lat", "lon"), P("lat"), P("lat"))
    return jax.shard_map(
        per_device,
        mesh=mesh,
        in_specs=placed,
        out_specs=(P(None, "lat", "lon"), P("lat", "lon"), P("lat", "lon")),
        check_vma=False,
    )
```

```python
import functools
import math

import jax
import jax.numpy as jnp
import numpy as np
from jax import lax
from jax.experimental import pallas as pl
from jax.experimental.pallas import tpu as pltpu
from jax.sharding import PartitionSpec as P

LEV = 8
LANES = 128
SUB = 8
UNIT = 4
MESH = pl.DeviceIdType.MESH
TABLES = 7
EXACT = lax.Precision.HIGHEST


def round_up(value, step):
    return -(-value // step) * step


def inner_length(columns):
    return max(a for a in range(1, LANES // LEV + 1) if columns % a == 0)


def halves(x):
    high = x.astype(jnp.bfloat16)
    return high, (x - high.astype(jnp.float32)).astype(jnp.bfloat16)


def left_dot(parts, x):
    high, low = halves(x)
    stacked = jnp.concatenate([high, low, high], axis=0)
    return jnp.dot(parts[...], stacked, preferred_element_type=jnp.float32)


def right_dot(x, parts):
    high, low = halves(x)
    stacked = jnp.concatenate([high, low, high], axis=1)
    return jnp.dot(stacked, parts[...], preferred_element_type=jnp.float32)


def dft_tables(length, inner):
    outer = length // inner
    half = outer // 2 + 1
    kept = round_up(half, SUB)
    p = np.arange(outer)
    k1 = np.arange(half)
    angle = 2.0 * np.pi * ((p[None, :] * k1[:, None]) % outer) / outer
    first = np.zeros((2 * kept, outer))
    first[:half] = np.cos(angle)
    first[kept : kept + half] = -np.sin(angle)
    twice = np.where((k1 == 0) | (2 * k1 == outer), 1.0, 2.0)[:, None] / length
    last = np.zeros((outer, 2 * kept))
    last[:, :half] = (twice * np.cos(angle)).T
    last[:, kept : kept + half] = (-twice * np.sin(angle)).T
    a = np.arange(inner)
    turn = 2.0 * np.pi * ((k1[:, None] * a[None, :]) % length) / length
    twiddle = np.zeros((2, kept, LANES))
    twiddle[0, :half, : inner * LEV] = np.repeat(np.cos(turn), LEV, axis=1)
    twiddle[1, :half, : inner * LEV] = np.repeat(-np.sin(turn), LEV, axis=1)
    small = 2.0 * np.pi * ((a[:, None] * a[None, :]) % inner) / inner
    eye = np.eye(LEV)

    def real_form(re, im):
        out = np.zeros((2 * LANES, 2 * LANES))
        used = inner * LEV
        out[:used, :used] = np.kron(re, eye)
        out[:used, LANES : LANES + used] = np.kron(im, eye)
        out[LANES : LANES + used, :used] = -np.kron(im, eye)
        out[LANES : LANES + used, LANES : LANES + used] = np.kron(re, eye)
        return out

    forward = real_form(np.cos(small), -np.sin(small))
    backward = real_form(np.cos(small), np.sin(small))
    k = k1[:, None] + outer * a[None, :]
    wave = np.zeros((kept, LANES))
    wave[:half, : inner * LEV] = np.repeat(np.minimum(k, length - k), LEV, axis=1)
    average = np.zeros((LANES, LANES))
    average[: inner * LEV, : inner * LEV] = np.kron(np.ones((inner, inner)), eye) / length

    def left_parts(table):
        high, low = halves(np.asarray(table, np.float32))
        return np.concatenate([high, high, low], axis=1)

    def right_parts(table):
        high, low = halves(np.asarray(table, np.float32))
        return np.concatenate([high, high, low], axis=0)

    matrices = [left_parts(first), right_parts(forward), right_parts(backward), left_parts(last)]
    return matrices + [np.asarray(t, np.float32) for t in (twiddle, wave, average)]


def plan(lat_size, lon_size, row_count):
    groups = row_count // UNIT
    turns = max(1, groups // lon_size)
    span = groups // turns
    split = lon_size // span
    planes = 1 if split == 4 else 2
    each = 4 // (planes * split)
    return groups, turns, span, split, planes, each


def filter_kernel(
    lat_size,
    lon_size,
    inner,
    winds,
    thickness,
    tracer,
    cutoff,
    damping,
    *rest,
):
    table_in, rest = rest[:TABLES], rest[TABLES:]
    filt, rest = rest[0], rest[1:]
    tables, rest = rest[:TABLES], rest[TABLES:]
    first, forward, backward, last, twiddle, wave, average = tables
    (

        recv,
    spread,
    done,
    ret,
    own,
    ext,
    edge,
    edge_in,
    prm,
    fwd_send,
    fwd_recv,
    ret_send,
    ret_recv,
    halo_send,
    halo_recv,
    rim_send,
    own_sem,
    edge_send,
    edge_recv,
    prm_sem,
    filt_sem,
    table_sem,
    ) = rest
    row_count, width = thickness.shape
    padded = filt.shape[-1]
    groups, turns, span, split, planes, each = plan(lat_size, lon_size, row_count)
    slots = turns * each
    used = inner * LEV
    pieces = width // used
    outer = pieces * lon_size
    kept = wave.shape[0]
    quarter = lat_size // 4
    bit = 1 << (lat_size.bit_length() - 3)
    polar_bands = [b for b in range(lat_size) if b < quarter or b >= lat_size - quarter]
    band = lax.axis_index("lat")
    lon = lax.axis_index("lon")
    is_polar = (band < quarter) | (band >= lat_size - quarter)
    lowbit = (band // bit) % 2
    partner = band + bit - 2 * bit * lowbit
    home = jnp.where(is_polar, band, partner)
    my_plane = jnp.where(is_polar, 0, 1)
    my_place = lax.rem(lon, span)
    my_split = lon // span

    def pair_of(b):
        return {b, b ^ bit} if planes == 2 else {b}

    linked = [[False] * lat_size for _ in range(lat_size)]
    for b in range(lat_size):
        linked[b][b] = True
    for pb in polar_bands:
        for worker in pair_of(pb):
            targets = pair_of(pb) | {t for t in (pb - 1, pb + 1) if 0 <= t < lat_size}
            for target in targets:
                linked[worker][target] = linked[target][worker] = True

    table_loads = [
        pltpu.make_async_copy(table_in[i], tables[i], table_sem.at[i]) for i in range(TABLES)
    ]
    arrays = [winds.at[0], winds.at[1], thickness, tracer]
    loads = [pltpu.make_async_copy(arrays[f], own.at[f], own_sem.at[f]) for f in range(4)]
    for load in loads + table_loads:
        load.start()
    barrier = pltpu.get_barrier_semaphore()
    expected = jnp.int32(-1)
    for other in range(lat_size):
        who = [b for b in range(lat_size) if linked[b][other]]
        talks = functools.reduce(jnp.logical_or, [band == b for b in who])
        expected += jnp.where(talks, lon_size, 0)

        @pl.when(talks)
        def _():
            for step in range(lon_size):
                target = lax.rem(lon + step, lon_size)

                @pl.when((target != lon) | (band != other))
                def _():
                    pl.semaphore_signal(
                        barrier, inc=1, device_id={"lat": other, "lon": target}, device_id_type=MESH
                    )

        near = [b for b in range(lat_size) if abs(b - other) == 1 and not linked[b][other]]
        if near:
            beside = functools.reduce(jnp.logical_or, [band == b for b in near])
            expected += jnp.where(beside, 1, 0)

            @pl.when(beside)
            def _():
                pl.semaphore_signal(
                    barrier, inc=1, device_id={"lat": other, "lon": lon}, device_id_type=MESH
                )

    pl.semaphore_wait(barrier, expected)

    def copies(src, dst, ssem, rsem, lat_to, lon_to):
        remote = pltpu.make_async_remote_copy(
            src_ref=src,
            dst_ref=dst,
            send_sem=ssem,
            recv_sem=rsem,
            device_id={"lat": lat_to, "lon": lon_to},
            device_id_type=MESH,
        )
        local = pltpu.make_async_copy(src, dst, rsem)
        return remote, local

    def push(src, dst, ssem, rsem, lat_to, lon_to):
        remote, local = copies(src, dst, ssem, rsem, lat_to, lon_to)
        same = (lat_to == band) & (lon_to == lon)

        @pl.when(same)
        def _():
            local.start()

        @pl.when(jnp.logical_not(same))
        def _():
            remote.start()

    def sent(src, dst, ssem, rsem, lat_to, lon_to):
        remote, _ = copies(src, dst, ssem, rsem, lat_to, lon_to)
        same = (lat_to == band) & (lon_to == lon)

        @pl.when(jnp.logical_not(same))
        def _():
            remote.wait_send()

    def arrived(dst, rsem):
        pltpu.make_async_copy(dst, dst, rsem).wait()

    def forward_copies(slot, action):
        turn = slot % turns
        for step in range(span):
            place = lax.rem(lon + step, span)
            for part in range(split):
                for plane in reversed(range(planes)):
                    target = part * span + place
                    field = (plane * split + part) * each + slot // turns
                    action(
                        ext.at[1 + turn * span + place, field],
                        recv.at[slot, lon],
                        fwd_send.at[slot, plane, target],
                        fwd_recv.at[slot, lon],
                        partner if plane else band,
                        target,
                    )

    def stage(field, turn):
        def one(i, carry):
            tile = turn * (span * UNIT // SUB) + i
            rows = own[field, pl.ds(pl.multiple_of(tile * SUB, SUB), SUB), :]
            for part in range(SUB // UNIT):
                block = rows[part * UNIT : (part + 1) * UNIT]
                ext[1 + tile * (SUB // UNIT) + part, field, :, :width] = block
            return carry

        lax.fori_loop(0, span * UNIT // SUB, one, 0)

    def stage_slot(slot):
        for lane in range(planes * split):
            stage(lane * each + slot // turns, slot % turns)

    for load in loads:
        load.wait()

    def param_copy():
        return pltpu.make_async_remote_copy(
            src_ref=prm,
            dst_ref=prm,
            send_sem=prm_sem.at[0],
            recv_sem=prm_sem.at[1],
            device_id={"lat": partner, "lon": lon},
            device_id_type=MESH,
        )

    @pl.when(is_polar)
    def _():
        stage_slot(0)
        forward_copies(0, push)
        for turn in range(turns):
            for j in range(UNIT):
                row = (turn * span + my_place) * UNIT + j
                low, high = j, UNIT + j
                prm[turn, low : low + 1] = jnp.full((1, LANES), cutoff[row].astype(jnp.float32))
                prm[turn, high : high + 1] = jnp.full((1, LANES), damping[row])
        for slot in range(1, slots):
            stage_slot(slot)
        if planes == 2:
            param_copy().start()

    def edge_copy(side):
        shift = 1 if side else lon_size - 1
        return pltpu.make_async_remote_copy(
            src_ref=edge,
            dst_ref=edge_in.at[side],
            send_sem=edge_send.at[side],
            recv_sem=edge_recv.at[side],
            device_id={"lat": band, "lon": lax.rem(lon + shift, lon_size)},
            device_id_type=MESH,
        )

    def rim_copy(side, item):
        return pltpu.make_async_remote_copy(
            src_ref=ext.at[1 if side == 0 else groups, item + 1],
            dst_ref=filt.at[groups + 1 if side == 0 else 0, item + 1],
            send_sem=rim_send.at[side, item],
            recv_sem=halo_recv.at[1 - side, item],
            device_id={"lat": band - 1 if side == 0 else band + 1, "lon": lon},
            device_id_type=MESH,
        )

    def keep_copy():
        inner_groups = pl.ds(1, groups)
        return pltpu.make_async_copy(ext.at[inner_groups], filt.at[inner_groups], filt_sem.at[0])

    @pl.when(jnp.logical_not(is_polar))
    def _():
        for field in range(4):
            for turn in range(turns):
                stage(field, turn)
        for item, f in enumerate((0, 2, 3)):
            edge[item, :, :, :LEV] = ext[1 : groups + 1, f, :, :LEV]
            edge[item, :, :, LEV : 2 * LEV] = ext[1 : groups + 1, f, :, width - LEV : width]
        edge_copy(0).start()
        edge_copy(1).start()
        edge_copy(0).wait()
        edge_copy(1).wait()
        for item, f in enumerate((0, 2, 3)):
            ext[1 : groups + 1, f, :, width : width + LEV] = edge_in[0, item, :, :, :LEV]
            ext[1 : groups + 1, f, :, padded - LEV :] = edge_in[1, item, :, :, LEV : 2 * LEV]
        keep_copy().start()
        for side in range(2):
            for item in range(3):
                rim_copy(side, item).start()

    def return_copies(slot, action):
        field = (my_plane * split + my_split) * each + slot // turns
        group = (slot % turns) * span + my_place
        for step in range(lon_size):
            target = lax.rem(lon + step, lon_size)
            action(
                ret.at[slot, target],
                filt.at[1 + group, field],
                ret_send.at[slot, target],
                ret_recv.at[slot, my_plane, lon],
                home,
                target,
            )
        item = jnp.maximum(field - 1, 0)
        opposite = lon_size // 2
        for side in range(2):
            if slot % turns != (0 if side == 0 else turns - 1):
                continue
            at_edge = group == (0 if side == 0 else groups - 1)
            at_pole = home == (0 if side == 0 else lat_size - 1)
            lat_to = home - 1 if side == 0 else home + 1

            @pl.when(at_edge & (field >= 1) & jnp.logical_not(at_pole))
            def _():
                for target in range(lon_size):
                    action(
                        ret.at[slot, target],
                        filt.at[groups + 1 if side == 0 else 0, item + 1],
                        halo_send.at[slot, side, target],
                        halo_recv.at[1 - side, item],
                        lat_to,
                        jnp.int32(target),
                    )

            @pl.when(at_edge & (field == 2) & at_pole)
            def _():
                for target in range(lon_size):
                    action(
                        ret.at[slot, target],
                        filt.at[0 if side == 0 else groups + 1, 2],
                        halo_send.at[slot, side, target],
                        halo_recv.at[side, 1],
                        home,
                        jnp.int32((target + opposite) % lon_size),
                    )

    batch = UNIT

    def work(slot):
        for s in range(lon_size):
            arrived(recv.at[slot, s], fwd_recv.at[slot, s])

        def spread_sector(s, carry):
            block = recv[slot, s]
            for p in range(pieces):
                piece = block[:, used * p : used * (p + 1)]
                if used < LANES:
                    blank = jnp.zeros((UNIT, LANES - used), jnp.float32)
                    piece = jnp.concatenate([piece, blank], axis=1)
                spread[pl.ds(s * pieces + p, UNIT, stride=outer), :] = piece
            return carry

        lax.fori_loop(0, lon_size, spread_sector, 0)

        def some_rows():
            base = 0
            rows = [spread[pl.ds((base + j) * outer, outer), :] for j in range(batch)]
            sums = [jnp.sum(row, axis=0, keepdims=True) for row in rows] * (SUB // batch)
            mean = jnp.dot(
                jnp.concatenate(sums, axis=0),
                average[...],
                precision=EXACT,
                preferred_element_type=jnp.float32,
            )
            means = [mean[j : j + 1] for j in range(batch)]
            x = jnp.concatenate([rows[j] - means[j] for j in range(batch)], axis=1)
            y = left_dot(first, x)
            tr, ti = twiddle[0], twiddle[1]
            z = []
            for j in range(batch):
                yr = y[:kept, j * LANES : (j + 1) * LANES]
                yi = y[kept:, j * LANES : (j + 1) * LANES]
                z.append(jnp.concatenate([yr * tr - yi * ti, yr * ti + yi * tr], axis=1))
            z = jnp.concatenate(z, axis=0)
            spectrum = right_dot(z, forward)
            k = wave[...]
            inverse_k = 1.0 / jnp.maximum(k, 1.0)
            weighted = []
            for j in range(batch):
                cut = prm[slot % turns, j : j + 1]
                damp = prm[slot % turns, UNIT + j : UNIT + j + 1]
                ratio = cut * inverse_k
                factor = jnp.where(k > cut, damp * ratio * ratio, 1.0)
                weighted.append(
                    spectrum[j * kept : (j + 1) * kept] * jnp.concatenate([factor, factor], axis=1)
                )
            weighted = jnp.concatenate(weighted, axis=0)
            v = right_dot(weighted, backward)
            u = []
            for j in range(batch):
                vr = v[j * kept : (j + 1) * kept, :LANES]
                vi = v[j * kept : (j + 1) * kept, LANES:]
                u.append(jnp.concatenate([vr * tr + vi * ti, vi * tr - vr * ti], axis=0))
            u = jnp.concatenate(u, axis=1)
            out = left_dot(last, u)
            for j in range(batch):
                piece = out[:, j * LANES : (j + 1) * LANES] + means[j]
                done[pl.ds((base + j) * outer, outer), :] = piece

        some_rows()

        def gather_sector(s, carry):
            for p in range(pieces):
                piece = done[pl.ds(s * pieces + p, UNIT, stride=outer), :]
                ret[slot, s, :, used * p : used * (p + 1)] = piece[:, :used]
            east = lax.rem(s + 1, lon_size) * pieces
            west = lax.rem(s + lon_size - 1, lon_size) * pieces + pieces - 1
            ret[slot, s, :, width : width + LEV] = done[pl.ds(east, UNIT, stride=outer), :][:, :LEV]
            ret[slot, s, :, padded - LEV :] = done[pl.ds(west, UNIT, stride=outer), :][
                :, used - LEV : used
            ]
            return carry

        lax.fori_loop(0, lon_size, gather_sector, 0)
        return_copies(slot, push)

    def all_work():
        for slot in range(slots):
            if slot + 1 < slots:

                @pl.when(is_polar)
                def _():
                    forward_copies(slot, sent)
                    forward_copies(slot + 1, push)

            work(slot)
        for slot in range(slots):
            return_copies(slot, sent)

    for load in table_loads:
        load.wait()

    if planes == 2:

        @pl.when(jnp.logical_not(is_polar))
        def _():
            param_copy().wait_recv()

        all_work()
    else:
        pl.when(is_polar)(all_work)

    @pl.when(is_polar)
    def _():
        if planes == 2:
            param_copy().wait_send()
        forward_copies(slots - 1, sent)
        for slot in range(slots):
            for plane in range(planes):
                for source in range(lon_size):
                    field = (plane * split + source // span) * each + slot // turns
                    group = (slot % turns) * span + source % span
                    arrived(filt.at[1 + group, field], ret_recv.at[slot, plane, source])

    @pl.when(jnp.logical_not(is_polar))
    def _():
        keep_copy().wait()
        for side in range(2):
            for item in range(3):
                rim_copy(side, item).wait_send()

    for side, rim in enumerate((0, groups + 1)):
        at_pole = band == (0 if side == 0 else lat_size - 1)
        arrived(filt.at[rim, 2], halo_recv.at[side, 1])

        @pl.when(jnp.logical_not(at_pole))
        def _():
            arrived(filt.at[rim, 1], halo_recv.at[side, 0])
            arrived(filt.at[rim, 3], halo_recv.at[side, 2])


def stencil_kernel(steps, lat_size, ratio, where_ref, below, *rest):
    parts = SUB // UNIT
    here, above, coef, uv, new_h, new_q = rest[:parts], *rest[parts:]
    step = pl.program_id(0)
    band = where_ref[0]
    width = new_h.shape[-1]
    padded = below.shape[-1]
    low_pole = (step == 0) & (band == 0)
    high_pole = (step == steps - 1) & (band == lat_size - 1)
    u, v, h, q = [jnp.concatenate([part[0, f] for part in here], axis=0) for f in range(4)]

    def south_of(x, f):
        row = below[0, f, UNIT - 1 : UNIT, :]
        pole = below[0, f, 0:1, :] if f == 2 else jnp.zeros_like(row)
        return jnp.concatenate([jnp.where(low_pole, pole, row), x[: SUB - 1]], axis=0)

    def north_of(x, f):
        row = above[0, f, 0:1, :]
        pole = above[0, f, UNIT - 1 : UNIT, :] if f == 2 else jnp.zeros_like(row)
        return jnp.concatenate([x[1:], jnp.where(high_pole, pole, row)], axis=0)

    def east_of(x):
        return pltpu.roll(x, padded - LEV, 1)

    def west_of(x):
        return pltpu.roll(x, LEV, 1)

    inv_c = coef[:, 0:1]
    face_s = coef[:, 1:2]
    face_n = coef[:, 2:3]
    he, hs, hn = east_of(h), south_of(h, 2), north_of(h, 2)
    hw = west_of(h)
    wind = 0.25 * (u + east_of(u))
    fx = wind * (h + he)
    gx = wind * (q + east_of(q))
    wind_s = face_s * (south_of(v, 1) + v)
    wind_n = face_n * (v + north_of(v, 1))
    fy = wind_n * (h + hn) - wind_s * (hs + h)
    gy = wind_n * (q + north_of(q, 3)) - wind_s * (south_of(q, 3) + q)
    out_h = h - ((fx - west_of(fx)) + fy) * inv_c
    out_q = q - ((gx - west_of(gx)) + gy) * inv_c
    out_u = u - (he - hw) * (0.5 * inv_c)
    out_v = v - (hn - hs) * (0.5 * ratio)
    uv[0] = out_u[:, :width]
    uv[1] = out_v[:, :width]
    new_h[...] = out_h[:, :width]
    new_q[...] = out_q[:, :width]


def per_device(winds, thickness, tracer, cutoff, damping):
    lat_size = lax.axis_size("lat")
    lon_size = lax.axis_size("lon")
    band = lax.axis_index("lat")
    row_count, width = thickness.shape
    columns = width // LEV
    length = columns * lon_size
    nlat = row_count * lat_size
    inner = inner_length(columns)
    outer = length // inner
    padded = round_up(width + 2 * LEV, LANES)
    groups, turns, span, split, planes, each = plan(lat_size, lon_size, row_count)
    slots = turns * each
    tables = [jnp.asarray(t) for t in dft_tables(length, inner)]
    vmem_spec = pl.BlockSpec(memory_space=pltpu.VMEM)
    hbm_spec = pl.BlockSpec(memory_space=pltpu.HBM)
    smem_spec = pl.BlockSpec(memory_space=pltpu.SMEM)
    f32 = jnp.float32
    filt = pl.pallas_call(
        functools.partial(filter_kernel, lat_size, lon_size, inner),
        out_shape=jax.ShapeDtypeStruct((groups + 2, 4, UNIT, padded), f32),
        in_specs=[hbm_spec] * 3 + [smem_spec] * 2 + [hbm_spec] * TABLES,
        out_specs=vmem_spec,
        scratch_shapes=[pltpu.VMEM(t.shape, t.dtype) for t in tables]
        + [
            pltpu.VMEM((slots, lon_size, UNIT, padded), f32),
            pltpu.VMEM((UNIT * outer, LANES), f32),
            pltpu.VMEM((UNIT * outer, LANES), f32),
            pltpu.VMEM((slots, lon_size, UNIT, padded), f32),
            pltpu.VMEM((4, row_count, width), f32),
            pltpu.VMEM((groups + 2, 4, UNIT, padded), f32),
            pltpu.VMEM((3, groups, UNIT, LANES), f32),
            pltpu.VMEM((2, 3, groups, UNIT, LANES), f32),
            pltpu.VMEM((turns, 2 * UNIT, LANES), f32),
            pltpu.SemaphoreType.DMA((slots, planes, lon_size)),
            pltpu.SemaphoreType.DMA((slots, lon_size)),
            pltpu.SemaphoreType.DMA((slots, lon_size)),
            pltpu.SemaphoreType.DMA((slots, 2, lon_size)),
            pltpu.SemaphoreType.DMA((slots, 2, lon_size)),
            pltpu.SemaphoreType.DMA((2, 3)),
            pltpu.SemaphoreType.DMA((2, 3)),
            pltpu.SemaphoreType.DMA((4,)),
            pltpu.SemaphoreType.DMA((2,)),
            pltpu.SemaphoreType.DMA((2,)),
            pltpu.SemaphoreType.DMA((2,)),
            pltpu.SemaphoreType.DMA((1,)),
            pltpu.SemaphoreType.DMA((TABLES,)),
        ],
        compiler_params=pltpu.CompilerParams(
            collective_id=0, has_side_effects=True, vmem_limit_bytes=54 * 1024 * 1024
        ),
        cost_estimate=pl.CostEstimate(
            flops=4 * 10**9, bytes_accessed=4 * row_count * padded * 8, transcendentals=0
        ),
        name="polar_filter",
    )(winds, thickness, tracer, cutoff, damping, *tables)

    dlam = 2.0 * math.pi / length
    dphi = math.pi / nlat
    ratio = dlam / dphi
    centers = np.cos(-np.pi / 2 + (np.arange(nlat) + 0.5) * dphi)
    faces = np.cos(-np.pi / 2 + np.arange(nlat + 1) * dphi)
    faces[0] = faces[-1] = 0.0
    faces = 0.25 * ratio * faces
    coef = jnp.asarray(np.stack([1.0 / centers, faces[:-1], faces[1:]], axis=1), f32)
    steps = row_count // SUB
    where_am_i = band.astype(jnp.int32).reshape(1)
    block = (1, 4, UNIT, padded)

    def block_of(part, i, b):
        return (i * (SUB // UNIT) + part, 0, 0, 0)

    uv, new_h, new_q = pl.pallas_call(
        functools.partial(stencil_kernel, steps, lat_size, ratio),
        grid_spec=pltpu.PrefetchScalarGridSpec(
            num_scalar_prefetch=1,
            grid=(steps,),
            in_specs=[
                pl.BlockSpec(block, functools.partial(block_of, part))
                for part in range(SUB // UNIT + 2)
            ]
            + [
                pl.BlockSpec((SUB, 3), lambda i, b: (b[0] * steps + i, 0)),
            ],
            out_specs=(
                pl.BlockSpec((2, SUB, width), lambda i, b: (0, i, 0)),
                pl.BlockSpec((SUB, width), lambda i, b: (i, 0)),
                pl.BlockSpec((SUB, width), lambda i, b: (i, 0)),
            ),
        ),
        out_shape=(
            jax.ShapeDtypeStruct((2, row_count, width), f32),
            jax.ShapeDtypeStruct((row_count, width), f32),
            jax.ShapeDtypeStruct((row_count, width), f32),
        ),
        compiler_params=pltpu.CompilerParams(vmem_limit_bytes=20 * 1024 * 1024),
        name="stencil",
    )(where_am_i, *[filt] * (SUB // UNIT + 2), coef)
    return uv, new_h, new_q


def solution(mesh):
    placed = (P(None, "lat", "lon"), P("lat", "lon"), P("lat", "lon"), P("lat"), P("lat"))
    return jax.shard_map(
        per_device,
        mesh=mesh,
        in_specs=placed,
        out_specs=(P(None, "lat", "lon"), P("lat", "lon"), P("lat", "lon")),
        check_vma=False,
    )
```

```python
import functools
import math

import jax
import jax.numpy as jnp
import numpy as np
from jax import lax
from jax.experimental import pallas as pl
from jax.experimental.pallas import tpu as pltpu
from jax.sharding import PartitionSpec as P

LEV = 8
LANES = 128
SUB = 8
UNIT = 4
MESH = pl.DeviceIdType.MESH
TABLES = 7
EXACT = lax.Precision.HIGHEST


def round_up(value, step):
    return -(-value // step) * step


def inner_length(columns):
    return max(a for a in range(1, LANES // LEV + 1) if columns % a == 0)


def halves(x):
    high = x.astype(jnp.bfloat16)
    return high, (x - high.astype(jnp.float32)).astype(jnp.bfloat16)


def left_dot(parts, x):
    high, low = halves(x)
    stacked = jnp.concatenate([high, low, high], axis=0)
    return jnp.dot(parts[...], stacked, preferred_element_type=jnp.float32)


def right_dot(x, parts):
    high, low = halves(x)
    stacked = jnp.concatenate([high, low, high], axis=1)
    return jnp.dot(stacked, parts[...], preferred_element_type=jnp.float32)


def dft_tables(length, inner):
    outer = length // inner
    half = outer // 2 + 1
    kept = round_up(half, SUB)
    p = np.arange(outer)
    k1 = np.arange(half)
    angle = 2.0 * np.pi * ((p[None, :] * k1[:, None]) % outer) / outer
    first = np.zeros((2 * kept, outer))
    first[:half] = np.cos(angle)
    first[kept : kept + half] = -np.sin(angle)
    twice = np.where((k1 == 0) | (2 * k1 == outer), 1.0, 2.0)[:, None] / length
    last = np.zeros((outer, 2 * kept))
    last[:, :half] = (twice * np.cos(angle)).T
    last[:, kept : kept + half] = (-twice * np.sin(angle)).T
    a = np.arange(inner)
    turn = 2.0 * np.pi * ((k1[:, None] * a[None, :]) % length) / length
    twiddle = np.zeros((2, kept, LANES))
    twiddle[0, :half, : inner * LEV] = np.repeat(np.cos(turn), LEV, axis=1)
    twiddle[1, :half, : inner * LEV] = np.repeat(-np.sin(turn), LEV, axis=1)
    small = 2.0 * np.pi * ((a[:, None] * a[None, :]) % inner) / inner
    eye = np.eye(LEV)

    def real_form(re, im):
        out = np.zeros((2 * LANES, 2 * LANES))
        used = inner * LEV
        out[:used, :used] = np.kron(re, eye)
        out[:used, LANES : LANES + used] = np.kron(im, eye)
        out[LANES : LANES + used, :used] = -np.kron(im, eye)
        out[LANES : LANES + used, LANES : LANES + used] = np.kron(re, eye)
        return out

    forward = real_form(np.cos(small), -np.sin(small))
    backward = real_form(np.cos(small), np.sin(small))
    k = k1[:, None] + outer * a[None, :]
    wave = np.zeros((kept, LANES))
    wave[:half, : inner * LEV] = np.repeat(np.minimum(k, length - k), LEV, axis=1)
    average = np.zeros((LANES, LANES))
    average[: inner * LEV, : inner * LEV] = np.kron(np.ones((inner, inner)), eye) / length

    def left_parts(table):
        high, low = halves(np.asarray(table, np.float32))
        return np.concatenate([high, high, low], axis=1)

    def right_parts(table):
        high, low = halves(np.asarray(table, np.float32))
        return np.concatenate([high, high, low], axis=0)

    matrices = [left_parts(first), right_parts(forward), right_parts(backward), left_parts(last)]
    return matrices + [np.asarray(t, np.float32) for t in (twiddle, wave, average)]


def plan(lat_size, lon_size, row_count):
    groups = row_count // UNIT
    turns = max(1, groups // lon_size)
    span = groups // turns
    split = lon_size // span
    jobs = []
    for field in range(0, 4, split):
        jobs += [(tuple(range(field, field + split)), turn) for turn in range(turns)]
    lent = 3 * len(jobs) // 8 if split == 1 else len(jobs) // 2
    return groups, turns, span, split, jobs[: len(jobs) - lent], jobs[len(jobs) - lent :]


def filter_kernel(
    lat_size,
    lon_size,
    inner,
    winds,
    thickness,
    tracer,
    cutoff,
    damping,
    *rest,
):
    table_in, rest = rest[:TABLES], rest[TABLES:]
    filt, rest = rest[0], rest[1:]
    tables, rest = rest[:TABLES], rest[TABLES:]
    first, forward, backward, last, twiddle, wave, average = tables
    (

        relay,
    recv,
    spread,
    done,
    ret,
    own,
    ext,
    edge,
    edge_in,
    prm,
    relay_send,
    relay_recv,
    fwd_send,
    fwd_recv,
    ret_send,
    ret_recv,
    halo_send,
    halo_recv,
    rim_send,
    own_sem,
    edge_send,
    edge_recv,
    prm_sem,
    filt_sem,
    table_sem,
    ) = rest
    row_count, width = thickness.shape
    padded = filt.shape[-1]
    groups, turns, span, split, kept_jobs, lent_jobs = plan(lat_size, lon_size, row_count)
    planes = 2 if lent_jobs else 1
    used = inner * LEV
    pieces = width // used
    outer = pieces * lon_size
    kept = wave.shape[0]
    quarter = lat_size // 4
    bit = 1 << (lat_size.bit_length() - 3)
    polar_bands = [b for b in range(lat_size) if b < quarter or b >= lat_size - quarter]
    band = lax.axis_index("lat")
    lon = lax.axis_index("lon")
    is_polar = (band < quarter) | (band >= lat_size - quarter)
    lowbit = (band // bit) % 2
    partner = band + bit - 2 * bit * lowbit
    home = jnp.where(is_polar, band, partner)
    my_plane = jnp.where(is_polar, 0, 1)
    my_place = lax.rem(lon, span)
    my_split = lon // span

    def pair_of(b):
        return {b, b ^ bit} if planes == 2 else {b}

    linked = [[False] * lat_size for _ in range(lat_size)]
    for b in range(lat_size):
        linked[b][b] = True
    for pb in polar_bands:
        for worker in pair_of(pb):
            targets = pair_of(pb) | {t for t in (pb - 1, pb + 1) if 0 <= t < lat_size}
            for target in targets:
                linked[worker][target] = linked[target][worker] = True

    table_loads = [
        pltpu.make_async_copy(table_in[i], tables[i], table_sem.at[i]) for i in range(TABLES)
    ]
    arrays = [winds.at[0], winds.at[1], thickness, tracer]
    loads = [pltpu.make_async_copy(arrays[f], own.at[f], own_sem.at[f]) for f in range(4)]
    for load in loads + table_loads:
        load.start()
    barrier = pltpu.get_barrier_semaphore()
    expected = jnp.int32(-1)
    for other in range(lat_size):
        who = [b for b in range(lat_size) if linked[b][other]]
        talks = functools.reduce(jnp.logical_or, [band == b for b in who])
        expected += jnp.where(talks, lon_size, 0)

        @pl.when(talks)
        def _():
            for step in range(lon_size):
                target = lax.rem(lon + step, lon_size)

                @pl.when((target != lon) | (band != other))
                def _():
                    pl.semaphore_signal(
                        barrier, inc=1, device_id={"lat": other, "lon": target}, device_id_type=MESH
                    )

        near = [b for b in range(lat_size) if abs(b - other) == 1 and not linked[b][other]]
        if near:
            beside = functools.reduce(jnp.logical_or, [band == b for b in near])
            expected += jnp.where(beside, 1, 0)

            @pl.when(beside)
            def _():
                pl.semaphore_signal(
                    barrier, inc=1, device_id={"lat": other, "lon": lon}, device_id_type=MESH
                )

    pl.semaphore_wait(barrier, expected)

    def copies(src, dst, ssem, rsem, lat_to, lon_to):
        remote = pltpu.make_async_remote_copy(
            src_ref=src,
            dst_ref=dst,
            send_sem=ssem,
            recv_sem=rsem,
            device_id={"lat": lat_to, "lon": lon_to},
            device_id_type=MESH,
        )
        local = pltpu.make_async_copy(src, dst, rsem)
        return remote, local

    def push(src, dst, ssem, rsem, lat_to, lon_to):
        remote, local = copies(src, dst, ssem, rsem, lat_to, lon_to)
        same = (lat_to == band) & (lon_to == lon)

        @pl.when(same)
        def _():
            local.start()

        @pl.when(jnp.logical_not(same))
        def _():
            remote.start()

    def sent(src, dst, ssem, rsem, lat_to, lon_to):
        remote, _ = copies(src, dst, ssem, rsem, lat_to, lon_to)
        same = (lat_to == band) & (lon_to == lon)

        @pl.when(jnp.logical_not(same))
        def _():
            remote.wait_send()

    def arrived(dst, rsem):
        pltpu.make_async_copy(dst, dst, rsem).wait()

    def own_copies(slot, action):
        fields, turn = kept_jobs[slot]
        for step in range(span):
            place = lax.rem(lon + step, span)
            for part in range(split):
                target = part * span + place
                action(
                    ext.at[1 + turn * span + place, fields[part]],
                    recv.at[slot, lon],
                    fwd_send.at[slot, target],
                    fwd_recv.at[slot, lon],
                    band,
                    target,
                )

    def relay_copies(slot):
        fields, turn = lent_jobs[slot]
        return [
            pltpu.make_async_remote_copy(
                src_ref=ext.at[pl.ds(1 + turn * span, span), fields[part]],
                dst_ref=relay.at[slot, part],
                send_sem=relay_send.at[slot, part],
                recv_sem=relay_recv.at[slot, part],
                device_id={"lat": partner, "lon": lon},
                device_id_type=MESH,
            )
            for part in range(split)
        ]

    def spread_copies(slot, action):
        for step in range(span):
            place = lax.rem(lon + step, span)
            for part in range(split):
                target = part * span + place
                action(
                    relay.at[slot, part, place],
                    recv.at[slot, lon],
                    fwd_send.at[slot, target],
                    fwd_recv.at[slot, lon],
                    band,
                    target,
                )

    def relayed(slot):
        for copy in relay_copies(slot):
            copy.wait_recv()
        spread_copies(slot, push)

    def stage(field, turn):
        def one(i, carry):
            tile = turn * (span * UNIT // SUB) + i
            rows = own[field, pl.ds(pl.multiple_of(tile * SUB, SUB), SUB), :]
            for part in range(SUB // UNIT):
                block = rows[part * UNIT : (part + 1) * UNIT]
                ext[1 + tile * (SUB // UNIT) + part, field, :, :width] = block
            return carry

        lax.fori_loop(0, span * UNIT // SUB, one, 0)

    def stage_job(job):
        for field in job[0]:
            stage(field, job[1])

    for load in loads:
        load.wait()

    def param_copy():
        return pltpu.make_async_remote_copy(
            src_ref=prm,
            dst_ref=prm,
            send_sem=prm_sem.at[0],
            recv_sem=prm_sem.at[1],
            device_id={"lat": partner, "lon": lon},
            device_id_type=MESH,
        )

    @pl.when(is_polar)
    def _():
        for job in lent_jobs[:1]:
            stage_job(job)
            for copy in relay_copies(0):
                copy.start()
        stage_job(kept_jobs[0])
        own_copies(0, push)
        for turn in range(turns):
            for j in range(UNIT):
                row = (turn * span + my_place) * UNIT + j
                low, high = j, UNIT + j
                prm[turn, low : low + 1] = jnp.full((1, LANES), cutoff[row].astype(jnp.float32))
                prm[turn, high : high + 1] = jnp.full((1, LANES), damping[row])
        for job in kept_jobs[1:] + lent_jobs[1:]:
            stage_job(job)
        if planes == 2:
            param_copy().start()

    def edge_copy(side):
        shift = 1 if side else lon_size - 1
        return pltpu.make_async_remote_copy(
            src_ref=edge,
            dst_ref=edge_in.at[side],
            send_sem=edge_send.at[side],
            recv_sem=edge_recv.at[side],
            device_id={"lat": band, "lon": lax.rem(lon + shift, lon_size)},
            device_id_type=MESH,
        )

    def rim_copy(side, item):
        return pltpu.make_async_remote_copy(
            src_ref=ext.at[1 if side == 0 else groups, item + 1],
            dst_ref=filt.at[groups + 1 if side == 0 else 0, item + 1],
            send_sem=rim_send.at[side, item],
            recv_sem=halo_recv.at[1 - side, item],
            device_id={"lat": band - 1 if side == 0 else band + 1, "lon": lon},
            device_id_type=MESH,
        )

    def keep_copy():
        inner_groups = pl.ds(1, groups)
        return pltpu.make_async_copy(ext.at[inner_groups], filt.at[inner_groups], filt_sem.at[0])

    @pl.when(jnp.logical_not(is_polar))
    def _():
        for field in range(4):
            for turn in range(turns):
                stage(field, turn)
        for item, f in enumerate((0, 2, 3)):
            edge[item, :, :, :LEV] = ext[1 : groups + 1, f, :, :LEV]
            edge[item, :, :, LEV : 2 * LEV] = ext[1 : groups + 1, f, :, width - LEV : width]
        edge_copy(0).start()
        edge_copy(1).start()
        edge_copy(0).wait()
        edge_copy(1).wait()
        for item, f in enumerate((0, 2, 3)):
            ext[1 : groups + 1, f, :, width : width + LEV] = edge_in[0, item, :, :, :LEV]
            ext[1 : groups + 1, f, :, padded - LEV :] = edge_in[1, item, :, :, LEV : 2 * LEV]
        keep_copy().start()
        for side in range(2):
            for item in range(3):
                rim_copy(side, item).start()

    def job_of(slot):
        def pick(jobs):
            fields, turn = jobs[min(slot, len(jobs) - 1)]
            field = jnp.int32(fields[0])
            for part in range(1, split):
                field = jnp.where(my_split == part, fields[part], field)
            return field, jnp.int32(turn)

        field, turn = pick(kept_jobs)
        if lent_jobs:
            lent_field, lent_turn = pick(lent_jobs)
            field = jnp.where(is_polar, field, lent_field)
            turn = jnp.where(is_polar, turn, lent_turn)
        return field, turn

    def return_copies(slot, action):
        field, turn = job_of(slot)
        group = turn * span + my_place
        for step in range(lon_size):
            target = lax.rem(lon + step, lon_size)
            action(
                ret.at[slot, target],
                filt.at[1 + group, field],
                ret_send.at[slot, target],
                ret_recv.at[slot, my_plane, lon],
                home,
                target,
            )
        item = jnp.maximum(field - 1, 0)
        opposite = lon_size // 2
        for side in range(2):
            at_edge = group == (0 if side == 0 else groups - 1)
            at_pole = home == (0 if side == 0 else lat_size - 1)
            lat_to = home - 1 if side == 0 else home + 1

            @pl.when(at_edge & (field >= 1) & jnp.logical_not(at_pole))
            def _():
                for target in range(lon_size):
                    action(
                        ret.at[slot, target],
                        filt.at[groups + 1 if side == 0 else 0, item + 1],
                        halo_send.at[slot, side, target],
                        halo_recv.at[1 - side, item],
                        lat_to,
                        jnp.int32(target),
                    )

            @pl.when(at_edge & (field == 2) & at_pole)
            def _():
                for target in range(lon_size):
                    action(
                        ret.at[slot, target],
                        filt.at[0 if side == 0 else groups + 1, 2],
                        halo_send.at[slot, side, target],
                        halo_recv.at[side, 1],
                        home,
                        jnp.int32((target + opposite) % lon_size),
                    )

    batch = UNIT

    def work(slot):
        _, turn = job_of(slot)
        for s in range(lon_size):
            arrived(recv.at[slot, s], fwd_recv.at[slot, s])

        def spread_sector(s, carry):
            block = recv[slot, s]
            for p in range(pieces):
                piece = block[:, used * p : used * (p + 1)]
                if used < LANES:
                    blank = jnp.zeros((UNIT, LANES - used), jnp.float32)
                    piece = jnp.concatenate([piece, blank], axis=1)
                spread[pl.ds(s * pieces + p, UNIT, stride=outer), :] = piece
            return carry

        lax.fori_loop(0, lon_size, spread_sector, 0)

        def some_rows():
            base = 0
            rows = [spread[pl.ds((base + j) * outer, outer), :] for j in range(batch)]
            sums = [jnp.sum(row, axis=0, keepdims=True) for row in rows] * (SUB // batch)
            mean = jnp.dot(
                jnp.concatenate(sums, axis=0),
                average[...],
                precision=EXACT,
                preferred_element_type=jnp.float32,
            )
            means = [mean[j : j + 1] for j in range(batch)]
            x = jnp.concatenate([rows[j] - means[j] for j in range(batch)], axis=1)
            y = left_dot(first, x)
            tr, ti = twiddle[0], twiddle[1]
            z = []
            for j in range(batch):
                yr = y[:kept, j * LANES : (j + 1) * LANES]
                yi = y[kept:, j * LANES : (j + 1) * LANES]
                z.append(jnp.concatenate([yr * tr - yi * ti, yr * ti + yi * tr], axis=1))
            z = jnp.concatenate(z, axis=0)
            spectrum = right_dot(z, forward)
            k = wave[...]
            inverse_k = 1.0 / jnp.maximum(k, 1.0)
            weighted = []
            for j in range(batch):
                cut = prm[turn, j : j + 1]
                damp = prm[turn, UNIT + j : UNIT + j + 1]
                ratio = cut * inverse_k
                factor = jnp.where(k > cut, damp * ratio * ratio, 1.0)
                weighted.append(
                    spectrum[j * kept : (j + 1) * kept] * jnp.concatenate([factor, factor], axis=1)
                )
            weighted = jnp.concatenate(weighted, axis=0)
            v = right_dot(weighted, backward)
            u = []
            for j in range(batch):
                vr = v[j * kept : (j + 1) * kept, :LANES]
                vi = v[j * kept : (j + 1) * kept, LANES:]
                u.append(jnp.concatenate([vr * tr + vi * ti, vi * tr - vr * ti], axis=0))
            u = jnp.concatenate(u, axis=1)
            out = left_dot(last, u)
            for j in range(batch):
                piece = out[:, j * LANES : (j + 1) * LANES] + means[j]
                done[pl.ds((base + j) * outer, outer), :] = piece

        some_rows()

        def gather_sector(s, carry):
            for p in range(pieces):
                piece = done[pl.ds(s * pieces + p, UNIT, stride=outer), :]
                ret[slot, s, :, used * p : used * (p + 1)] = piece[:, :used]
            east = lax.rem(s + 1, lon_size) * pieces
            west = lax.rem(s + lon_size - 1, lon_size) * pieces + pieces - 1
            ret[slot, s, :, width : width + LEV] = done[pl.ds(east, UNIT, stride=outer), :][:, :LEV]
            ret[slot, s, :, padded - LEV :] = done[pl.ds(west, UNIT, stride=outer), :][
                :, used - LEV : used
            ]
            return carry

        lax.fori_loop(0, lon_size, gather_sector, 0)
        return_copies(slot, push)

    for load in table_loads:
        load.wait()

    if lent_jobs:

        @pl.when(jnp.logical_not(is_polar))
        def _():
            param_copy().wait_recv()
            relayed(0)

    kept_count, lent_count = len(kept_jobs), len(lent_jobs)
    for slot in range(max(kept_count, lent_count)):

        @pl.when(is_polar)
        def _():
            if slot + 1 < kept_count:
                own_copies(slot, sent)
                own_copies(slot + 1, push)
            if slot >= 2 and slot < lent_count:
                for copy in relay_copies(slot - 2):
                    copy.wait_send()
                for copy in relay_copies(slot):
                    copy.start()
            if slot == 0 and lent_count > 1:
                for copy in relay_copies(1):
                    copy.start()

        if slot + 1 < lent_count:

            @pl.when(jnp.logical_not(is_polar))
            def _():
                relayed(slot + 1)

        if slot < kept_count and slot < lent_count:
            work(slot)
        elif slot < kept_count:
            pl.when(is_polar)(functools.partial(work, slot))
        else:
            pl.when(jnp.logical_not(is_polar))(functools.partial(work, slot))

    @pl.when(is_polar)
    def _():
        if lent_jobs:
            param_copy().wait_send()
            for slot in range(max(0, lent_count - 2), lent_count):
                for copy in relay_copies(slot):
                    copy.wait_send()
        own_copies(kept_count - 1, sent)
        for slot in range(kept_count):
            return_copies(slot, sent)
        for plane, jobs in enumerate((kept_jobs, lent_jobs)):
            for slot, (fields, turn) in enumerate(jobs):
                for source in range(lon_size):
                    group = turn * span + source % span
                    field = fields[source // span]
                    arrived(filt.at[1 + group, field], ret_recv.at[slot, plane, source])

    if lent_jobs:

        @pl.when(jnp.logical_not(is_polar))
        def _():
            for slot in range(lent_count):
                spread_copies(slot, sent)
                return_copies(slot, sent)

    @pl.when(jnp.logical_not(is_polar))
    def _():
        keep_copy().wait()
        for side in range(2):
            for item in range(3):
                rim_copy(side, item).wait_send()

    for side, rim in enumerate((0, groups + 1)):
        at_pole = band == (0 if side == 0 else lat_size - 1)
        arrived(filt.at[rim, 2], halo_recv.at[side, 1])

        @pl.when(jnp.logical_not(at_pole))
        def _():
            arrived(filt.at[rim, 1], halo_recv.at[side, 0])
            arrived(filt.at[rim, 3], halo_recv.at[side, 2])


def stencil_kernel(steps, lat_size, ratio, where_ref, below, *rest):
    parts = SUB // UNIT
    here, above, coef, uv, new_h, new_q = rest[:parts], *rest[parts:]
    step = pl.program_id(0)
    band = where_ref[0]
    width = new_h.shape[-1]
    padded = below.shape[-1]
    low_pole = (step == 0) & (band == 0)
    high_pole = (step == steps - 1) & (band == lat_size - 1)
    u, v, h, q = [jnp.concatenate([part[0, f] for part in here], axis=0) for f in range(4)]

    def south_of(x, f):
        row = below[0, f, UNIT - 1 : UNIT, :]
        pole = below[0, f, 0:1, :] if f == 2 else jnp.zeros_like(row)
        return jnp.concatenate([jnp.where(low_pole, pole, row), x[: SUB - 1]], axis=0)

    def north_of(x, f):
        row = above[0, f, 0:1, :]
        pole = above[0, f, UNIT - 1 : UNIT, :] if f == 2 else jnp.zeros_like(row)
        return jnp.concatenate([x[1:], jnp.where(high_pole, pole, row)], axis=0)

    def east_of(x):
        return pltpu.roll(x, padded - LEV, 1)

    def west_of(x):
        return pltpu.roll(x, LEV, 1)

    inv_c = coef[:, 0:1]
    face_s = coef[:, 1:2]
    face_n = coef[:, 2:3]
    he, hs, hn = east_of(h), south_of(h, 2), north_of(h, 2)
    hw = west_of(h)
    wind = 0.25 * (u + east_of(u))
    fx = wind * (h + he)
    gx = wind * (q + east_of(q))
    wind_s = face_s * (south_of(v, 1) + v)
    wind_n = face_n * (v + north_of(v, 1))
    fy = wind_n * (h + hn) - wind_s * (hs + h)
    gy = wind_n * (q + north_of(q, 3)) - wind_s * (south_of(q, 3) + q)
    out_h = h - ((fx - west_of(fx)) + fy) * inv_c
    out_q = q - ((gx - west_of(gx)) + gy) * inv_c
    out_u = u - (he - hw) * (0.5 * inv_c)
    out_v = v - (hn - hs) * (0.5 * ratio)
    uv[0] = out_u[:, :width]
    uv[1] = out_v[:, :width]
    new_h[...] = out_h[:, :width]
    new_q[...] = out_q[:, :width]


def per_device(winds, thickness, tracer, cutoff, damping):
    lat_size = lax.axis_size("lat")
    lon_size = lax.axis_size("lon")
    band = lax.axis_index("lat")
    row_count, width = thickness.shape
    columns = width // LEV
    length = columns * lon_size
    nlat = row_count * lat_size
    inner = inner_length(columns)
    outer = length // inner
    padded = round_up(width + 2 * LEV, LANES)
    groups, turns, span, split, kept_jobs, lent_jobs = plan(lat_size, lon_size, row_count)
    slots = max(len(kept_jobs), len(lent_jobs))
    relays = max(1, len(lent_jobs))
    tables = [jnp.asarray(t) for t in dft_tables(length, inner)]
    vmem_spec = pl.BlockSpec(memory_space=pltpu.VMEM)
    hbm_spec = pl.BlockSpec(memory_space=pltpu.HBM)
    smem_spec = pl.BlockSpec(memory_space=pltpu.SMEM)
    f32 = jnp.float32
    filt = pl.pallas_call(
        functools.partial(filter_kernel, lat_size, lon_size, inner),
        out_shape=jax.ShapeDtypeStruct((groups + 2, 4, UNIT, padded), f32),
        in_specs=[hbm_spec] * 3 + [smem_spec] * 2 + [hbm_spec] * TABLES,
        out_specs=vmem_spec,
        scratch_shapes=[pltpu.VMEM(t.shape, t.dtype) for t in tables]
        + [
            pltpu.VMEM((relays, split, span, UNIT, padded), f32),
            pltpu.VMEM((slots, lon_size, UNIT, padded), f32),
            pltpu.VMEM((UNIT * outer, LANES), f32),
            pltpu.VMEM((UNIT * outer, LANES), f32),
            pltpu.VMEM((slots, lon_size, UNIT, padded), f32),
            pltpu.VMEM((4, row_count, width), f32),
            pltpu.VMEM((groups + 2, 4, UNIT, padded), f32),
            pltpu.VMEM((3, groups, UNIT, LANES), f32),
            pltpu.VMEM((2, 3, groups, UNIT, LANES), f32),
            pltpu.VMEM((turns, 2 * UNIT, LANES), f32),
            pltpu.SemaphoreType.DMA((relays, split)),
            pltpu.SemaphoreType.DMA((relays, split)),
            pltpu.SemaphoreType.DMA((slots, lon_size)),
            pltpu.SemaphoreType.DMA((slots, lon_size)),
            pltpu.SemaphoreType.DMA((slots, lon_size)),
            pltpu.SemaphoreType.DMA((slots, 2, lon_size)),
            pltpu.SemaphoreType.DMA((slots, 2, lon_size)),
            pltpu.SemaphoreType.DMA((2, 3)),
            pltpu.SemaphoreType.DMA((2, 3)),
            pltpu.SemaphoreType.DMA((4,)),
            pltpu.SemaphoreType.DMA((2,)),
            pltpu.SemaphoreType.DMA((2,)),
            pltpu.SemaphoreType.DMA((2,)),
            pltpu.SemaphoreType.DMA((1,)),
            pltpu.SemaphoreType.DMA((TABLES,)),
        ],
        compiler_params=pltpu.CompilerParams(
            collective_id=0, has_side_effects=True, vmem_limit_bytes=54 * 1024 * 1024
        ),
        cost_estimate=pl.CostEstimate(
            flops=4 * 10**9, bytes_accessed=4 * row_count * padded * 8, transcendentals=0
        ),
        name="polar_filter",
    )(winds, thickness, tracer, cutoff, damping, *tables)

    dlam = 2.0 * math.pi / length
    dphi = math.pi / nlat
    ratio = dlam / dphi
    centers = np.cos(-np.pi / 2 + (np.arange(nlat) + 0.5) * dphi)
    faces = np.cos(-np.pi / 2 + np.arange(nlat + 1) * dphi)
    faces[0] = faces[-1] = 0.0
    faces = 0.25 * ratio * faces
    coef = jnp.asarray(np.stack([1.0 / centers, faces[:-1], faces[1:]], axis=1), f32)
    steps = row_count // SUB
    where_am_i = band.astype(jnp.int32).reshape(1)
    block = (1, 4, UNIT, padded)

    def block_of(part, i, b):
        return (i * (SUB // UNIT) + part, 0, 0, 0)

    uv, new_h, new_q = pl.pallas_call(
        functools.partial(stencil_kernel, steps, lat_size, ratio),
        grid_spec=pltpu.PrefetchScalarGridSpec(
            num_scalar_prefetch=1,
            grid=(steps,),
            in_specs=[
                pl.BlockSpec(block, functools.partial(block_of, part))
                for part in range(SUB // UNIT + 2)
            ]
            + [
                pl.BlockSpec((SUB, 3), lambda i, b: (b[0] * steps + i, 0)),
            ],
            out_specs=(
                pl.BlockSpec((2, SUB, width), lambda i, b: (0, i, 0)),
                pl.BlockSpec((SUB, width), lambda i, b: (i, 0)),
                pl.BlockSpec((SUB, width), lambda i, b: (i, 0)),
            ),
        ),
        out_shape=(
            jax.ShapeDtypeStruct((2, row_count, width), f32),
            jax.ShapeDtypeStruct((row_count, width), f32),
            jax.ShapeDtypeStruct((row_count, width), f32),
        ),
        compiler_params=pltpu.CompilerParams(vmem_limit_bytes=20 * 1024 * 1024),
        name="stencil",
    )(where_am_i, *[filt] * (SUB // UNIT + 2), coef)
    return uv, new_h, new_q


def solution(mesh):
    placed = (P(None, "lat", "lon"), P("lat", "lon"), P("lat", "lon"), P("lat"), P("lat"))
    return jax.shard_map(
        per_device,
        mesh=mesh,
        in_specs=placed,
        out_specs=(P(None, "lat", "lon"), P("lat", "lon"), P("lat", "lon")),
        check_vma=False,
    )
```

```python
import functools
import math

import jax
import jax.numpy as jnp
import numpy as np
from jax import lax
from jax.experimental import pallas as pl
from jax.experimental.pallas import tpu as pltpu
from jax.sharding import PartitionSpec as P

LEV = 8
LANES = 128
SUB = 8
UNIT = 4
MESH = pl.DeviceIdType.MESH
TABLES = 7


def round_up(value, step):
    return -(-value // step) * step


def halves(x):
    high = x.astype(jnp.bfloat16)
    return high, (x - high.astype(jnp.float32)).astype(jnp.bfloat16)


def left_dot(parts, x):
    high, low = halves(x)
    stacked = jnp.concatenate([high, low, high], axis=0)
    return jnp.dot(parts[...], stacked, preferred_element_type=jnp.float32)


def right_dot(x, parts):
    high, low = halves(x)
    stacked = jnp.concatenate([high, low, high], axis=1)
    return jnp.dot(stacked, parts[...], preferred_element_type=jnp.float32)


def dft_tables(length, inner):
    outer = length // inner
    depth = round_up(outer, 2 * SUB)
    half = outer // 2 + 1
    kept = round_up(half, SUB)
    p = np.arange(outer)
    k1 = np.arange(half)
    angle = 2.0 * np.pi * ((p[None, :] * k1[:, None]) % outer) / outer
    first = np.zeros((2 * kept, depth))
    first[:half, :outer] = np.cos(angle)
    first[kept : kept + half, :outer] = -np.sin(angle)
    twice = np.where((k1 == 0) | (2 * k1 == outer), 1.0, 2.0)[:, None] / length
    last = np.zeros((depth, 2 * kept))
    last[:outer, :half] = (twice * np.cos(angle)).T
    last[:outer, kept : kept + half] = (-twice * np.sin(angle)).T
    a = np.arange(inner)
    turn = 2.0 * np.pi * ((k1[:, None] * a[None, :]) % length) / length
    twiddle = np.zeros((2, kept, LANES))
    twiddle[0, :half, : inner * LEV] = np.repeat(np.cos(turn), LEV, axis=1)
    twiddle[1, :half, : inner * LEV] = np.repeat(-np.sin(turn), LEV, axis=1)
    small = 2.0 * np.pi * ((a[:, None] * a[None, :]) % inner) / inner
    eye = np.eye(LEV)

    def real_form(re, im):
        out = np.zeros((2 * LANES, 2 * LANES))
        used = inner * LEV
        out[:used, :used] = np.kron(re, eye)
        out[:used, LANES : LANES + used] = np.kron(im, eye)
        out[LANES : LANES + used, :used] = -np.kron(im, eye)
        out[LANES : LANES + used, LANES : LANES + used] = np.kron(re, eye)
        return out

    forward = real_form(np.cos(small), -np.sin(small))
    backward = real_form(np.cos(small), np.sin(small))
    k = k1[:, None] + outer * a[None, :]
    wave = np.zeros((kept, LANES))
    wave[:half, : inner * LEV] = np.repeat(np.minimum(k, length - k), LEV, axis=1)
    average = np.zeros((LANES, LANES))
    average[: inner * LEV, : inner * LEV] = np.kron(np.ones((inner, inner)), eye) / length

    def left_parts(table):
        high, low = halves(np.asarray(table, np.float32))
        return np.concatenate([high, high, low], axis=1)

    def right_parts(table):
        high, low = halves(np.asarray(table, np.float32))
        return np.concatenate([high, high, low], axis=0)

    matrices = [left_parts(first), right_parts(forward), right_parts(backward), left_parts(last)]
    return matrices + [np.asarray(t, np.float32) for t in (twiddle, wave, average)]


def plan(lat_size, lon_size, row_count):
    groups = row_count // UNIT
    turns = max(1, groups // lon_size)
    span = groups // turns
    split = lon_size // span
    jobs = []
    for field in range(0, 4, split):
        jobs += [(tuple(range(field, field + split)), turn) for turn in range(turns)]
    lent = 3 * len(jobs) // 8 if split == 1 else len(jobs) // 2
    return groups, turns, span, split, jobs[: len(jobs) - lent], jobs[len(jobs) - lent :]


def filter_kernel(
    lat_size,
    lon_size,
    winds,
    thickness,
    tracer,
    cutoff,
    damping,
    *rest,
):
    table_in, rest = rest[:TABLES], rest[TABLES:]
    filt, rest = rest[0], rest[1:]
    tables, rest = rest[:TABLES], rest[TABLES:]
    first, forward, backward, last, twiddle, wave, average = tables
    (

        relay,
    recv,
    spread,
    done,
    ret,
    own,
    ext,
    edge,
    edge_in,
    prm,
    relay_send,
    relay_recv,
    fwd_send,
    fwd_recv,
    ret_send,
    ret_recv,
    halo_send,
    halo_recv,
    rim_send,
    own_sem,
    edge_send,
    edge_recv,
    prm_sem,
    filt_sem,
    table_sem,
    ) = rest
    row_count, width = thickness.shape
    padded = filt.shape[-1]
    groups, turns, span, split, kept_jobs, lent_jobs = plan(lat_size, lon_size, row_count)
    planes = 2 if lent_jobs else 1
    outer = width * lon_size // LANES
    depth = first.shape[1] // 3
    period = math.lcm(width, LANES)
    near_sectors, near_tiles = period // width, period // LANES
    kept = wave.shape[0]
    quarter = lat_size // 4
    bit = 1 << (lat_size.bit_length() - 3)
    polar_bands = [b for b in range(lat_size) if b < quarter or b >= lat_size - quarter]
    band = lax.axis_index("lat")
    lon = lax.axis_index("lon")
    is_polar = (band < quarter) | (band >= lat_size - quarter)
    lowbit = (band // bit) % 2
    partner = band + bit - 2 * bit * lowbit
    home = jnp.where(is_polar, band, partner)
    my_plane = jnp.where(is_polar, 0, 1)
    my_place = lax.rem(lon, span)
    my_split = lon // span

    def pair_of(b):
        return {b, b ^ bit} if planes == 2 else {b}

    linked = [[False] * lat_size for _ in range(lat_size)]
    for b in range(lat_size):
        linked[b][b] = True
    for pb in polar_bands:
        for worker in pair_of(pb):
            targets = pair_of(pb) | {t for t in (pb - 1, pb + 1) if 0 <= t < lat_size}
            for target in targets:
                linked[worker][target] = linked[target][worker] = True

    table_loads = [
        pltpu.make_async_copy(table_in[i], tables[i], table_sem.at[i]) for i in range(TABLES)
    ]
    arrays = [winds.at[0], winds.at[1], thickness, tracer]
    loads = [pltpu.make_async_copy(arrays[f], own.at[f], own_sem.at[f]) for f in range(4)]
    for load in loads + table_loads:
        load.start()
    barrier = pltpu.get_barrier_semaphore()
    expected = jnp.int32(-1)
    for other in range(lat_size):
        who = [b for b in range(lat_size) if linked[b][other]]
        talks = functools.reduce(jnp.logical_or, [band == b for b in who])
        expected += jnp.where(talks, lon_size, 0)

        @pl.when(talks)
        def _():
            for step in range(lon_size):
                target = lax.rem(lon + step, lon_size)

                @pl.when((target != lon) | (band != other))
                def _():
                    pl.semaphore_signal(
                        barrier, inc=1, device_id={"lat": other, "lon": target}, device_id_type=MESH
                    )

        near = [b for b in range(lat_size) if abs(b - other) == 1 and not linked[b][other]]
        if near:
            beside = functools.reduce(jnp.logical_or, [band == b for b in near])
            expected += jnp.where(beside, 1, 0)

            @pl.when(beside)
            def _():
                pl.semaphore_signal(
                    barrier, inc=1, device_id={"lat": other, "lon": lon}, device_id_type=MESH
                )

    pl.semaphore_wait(barrier, expected)

    def copies(src, dst, ssem, rsem, lat_to, lon_to):
        remote = pltpu.make_async_remote_copy(
            src_ref=src,
            dst_ref=dst,
            send_sem=ssem,
            recv_sem=rsem,
            device_id={"lat": lat_to, "lon": lon_to},
            device_id_type=MESH,
        )
        local = pltpu.make_async_copy(src, dst, rsem)
        return remote, local

    def push(src, dst, ssem, rsem, lat_to, lon_to):
        remote, local = copies(src, dst, ssem, rsem, lat_to, lon_to)
        same = (lat_to == band) & (lon_to == lon)

        @pl.when(same)
        def _():
            local.start()

        @pl.when(jnp.logical_not(same))
        def _():
            remote.start()

    def sent(src, dst, ssem, rsem, lat_to, lon_to):
        remote, _ = copies(src, dst, ssem, rsem, lat_to, lon_to)
        same = (lat_to == band) & (lon_to == lon)

        @pl.when(jnp.logical_not(same))
        def _():
            remote.wait_send()

    def arrived(dst, rsem):
        pltpu.make_async_copy(dst, dst, rsem).wait()

    def own_copies(slot, action):
        fields, turn = kept_jobs[slot]
        for step in range(span):
            place = lax.rem(lon + step, span)
            for part in range(split):
                target = part * span + place
                action(
                    ext.at[1 + turn * span + place, fields[part]],
                    recv.at[slot, lon],
                    fwd_send.at[slot, target],
                    fwd_recv.at[slot, lon],
                    band,
                    target,
                )

    def relay_copies(slot):
        fields, turn = lent_jobs[slot]
        return [
            pltpu.make_async_remote_copy(
                src_ref=ext.at[pl.ds(1 + turn * span, span), fields[part]],
                dst_ref=relay.at[slot, part],
                send_sem=relay_send.at[slot, part],
                recv_sem=relay_recv.at[slot, part],
                device_id={"lat": partner, "lon": lon},
                device_id_type=MESH,
            )
            for part in range(split)
        ]

    def spread_copies(slot, action):
        for step in range(span):
            place = lax.rem(lon + step, span)
            for part in range(split):
                target = part * span + place
                action(
                    relay.at[slot, part, place],
                    recv.at[slot, lon],
                    fwd_send.at[slot, target],
                    fwd_recv.at[slot, lon],
                    band,
                    target,
                )

    def relayed(slot):
        for copy in relay_copies(slot):
            copy.wait_recv()
        spread_copies(slot, push)

    def stage(field, turn):
        def one(i, carry):
            tile = turn * (span * UNIT // SUB) + i
            rows = own[field, pl.ds(pl.multiple_of(tile * SUB, SUB), SUB), :]
            for part in range(SUB // UNIT):
                block = rows[part * UNIT : (part + 1) * UNIT]
                ext[1 + tile * (SUB // UNIT) + part, field, :, :width] = block
            return carry

        lax.fori_loop(0, span * UNIT // SUB, one, 0)

    def stage_job(job):
        for field in job[0]:
            stage(field, job[1])

    spread[...] = jnp.zeros_like(spread)
    for load in loads:
        load.wait()

    def param_copy():
        return pltpu.make_async_remote_copy(
            src_ref=prm,
            dst_ref=prm,
            send_sem=prm_sem.at[0],
            recv_sem=prm_sem.at[1],
            device_id={"lat": partner, "lon": lon},
            device_id_type=MESH,
        )

    @pl.when(is_polar)
    def _():
        for job in lent_jobs[:1]:
            stage_job(job)
            for copy in relay_copies(0):
                copy.start()
        stage_job(kept_jobs[0])
        own_copies(0, push)
        for turn in range(turns):
            for j in range(UNIT):
                row = (turn * span + my_place) * UNIT + j
                low, high = j, UNIT + j
                prm[turn, low : low + 1] = jnp.full((1, LANES), cutoff[row].astype(jnp.float32))
                prm[turn, high : high + 1] = jnp.full((1, LANES), damping[row])
        for job in kept_jobs[1:] + lent_jobs[1:]:
            stage_job(job)
        if planes == 2:
            param_copy().start()

    def edge_copy(side):
        shift = 1 if side else lon_size - 1
        return pltpu.make_async_remote_copy(
            src_ref=edge,
            dst_ref=edge_in.at[side],
            send_sem=edge_send.at[side],
            recv_sem=edge_recv.at[side],
            device_id={"lat": band, "lon": lax.rem(lon + shift, lon_size)},
            device_id_type=MESH,
        )

    def rim_copy(side, item):
        return pltpu.make_async_remote_copy(
            src_ref=ext.at[1 if side == 0 else groups, item + 1],
            dst_ref=filt.at[groups + 1 if side == 0 else 0, item + 1],
            send_sem=rim_send.at[side, item],
            recv_sem=halo_recv.at[1 - side, item],
            device_id={"lat": band - 1 if side == 0 else band + 1, "lon": lon},
            device_id_type=MESH,
        )

    def keep_copy():
        inner_groups = pl.ds(1, groups)
        return pltpu.make_async_copy(ext.at[inner_groups], filt.at[inner_groups], filt_sem.at[0])

    @pl.when(jnp.logical_not(is_polar))
    def _():
        for field in range(4):
            for turn in range(turns):
                stage(field, turn)
        for item, f in enumerate((0, 2, 3)):
            edge[item, :, :, :LEV] = ext[1 : groups + 1, f, :, :LEV]
            edge[item, :, :, LEV : 2 * LEV] = ext[1 : groups + 1, f, :, width - LEV : width]
        edge_copy(0).start()
        edge_copy(1).start()
        edge_copy(0).wait()
        edge_copy(1).wait()
        for item, f in enumerate((0, 2, 3)):
            ext[1 : groups + 1, f, :, width : width + LEV] = edge_in[0, item, :, :, :LEV]
            ext[1 : groups + 1, f, :, padded - LEV :] = edge_in[1, item, :, :, LEV : 2 * LEV]
        keep_copy().start()
        for side in range(2):
            for item in range(3):
                rim_copy(side, item).start()

    def job_of(slot):
        def pick(jobs):
            fields, turn = jobs[min(slot, len(jobs) - 1)]
            field = jnp.int32(fields[0])
            for part in range(1, split):
                field = jnp.where(my_split == part, fields[part], field)
            return field, jnp.int32(turn)

        field, turn = pick(kept_jobs)
        if lent_jobs:
            lent_field, lent_turn = pick(lent_jobs)
            field = jnp.where(is_polar, field, lent_field)
            turn = jnp.where(is_polar, turn, lent_turn)
        return field, turn

    def return_copies(slot, action):
        field, turn = job_of(slot)
        group = turn * span + my_place
        for step in range(lon_size):
            target = lax.rem(lon + step, lon_size)
            action(
                ret.at[slot, target],
                filt.at[1 + group, field],
                ret_send.at[slot, target],
                ret_recv.at[slot, my_plane, lon],
                home,
                target,
            )
        item = jnp.maximum(field - 1, 0)
        opposite = lon_size // 2
        for side in range(2):
            at_edge = group == (0 if side == 0 else groups - 1)
            at_pole = home == (0 if side == 0 else lat_size - 1)
            lat_to = home - 1 if side == 0 else home + 1

            @pl.when(at_edge & (field >= 1) & jnp.logical_not(at_pole))
            def _():
                for target in range(lon_size):
                    action(
                        ret.at[slot, target],
                        filt.at[groups + 1 if side == 0 else 0, item + 1],
                        halo_send.at[slot, side, target],
                        halo_recv.at[1 - side, item],
                        lat_to,
                        jnp.int32(target),
                    )

            @pl.when(at_edge & (field == 2) & at_pole)
            def _():
                for target in range(lon_size):
                    action(
                        ret.at[slot, target],
                        filt.at[0 if side == 0 else groups + 1, 2],
                        halo_send.at[slot, side, target],
                        halo_recv.at[side, 1],
                        home,
                        jnp.int32((target + opposite) % lon_size),
                    )

    batch = UNIT

    def work(slot):
        _, turn = job_of(slot)
        for s in range(lon_size):
            arrived(recv.at[slot, s], fwd_recv.at[slot, s])

        def spread_period(m, carry):
            for t in range(near_tiles):
                source, lane = divmod(t * LANES, width)
                take = min(LANES, width - lane)
                tile = recv[slot, m * near_sectors + source, :, lane : lane + take]
                if take < LANES:
                    more = recv[slot, m * near_sectors + source + 1, :, : LANES - take]
                    tile = jnp.concatenate([tile, more], axis=1)
                spread[pl.ds(m * near_tiles + t, UNIT, stride=depth), :] = tile
            return carry

        lax.fori_loop(0, lon_size // near_sectors, spread_period, 0)

        def some_rows():
            base = 0
            rows = [spread[pl.ds((base + j) * depth, depth), :] for j in range(batch)]
            sums = [jnp.sum(row, axis=0, keepdims=True) for row in rows] * (SUB // batch)
            mean = jnp.dot(
                jnp.concatenate(sums, axis=0),
                average[...],
                preferred_element_type=jnp.float32,
            )
            means = [mean[j : j + 1] for j in range(batch)]
            x = jnp.concatenate([rows[j] - means[j] for j in range(batch)], axis=1)
            y = left_dot(first, x)
            tr, ti = twiddle[0], twiddle[1]
            z = []
            for j in range(batch):
                yr = y[:kept, j * LANES : (j + 1) * LANES]
                yi = y[kept:, j * LANES : (j + 1) * LANES]
                z.append(jnp.concatenate([yr * tr - yi * ti, yr * ti + yi * tr], axis=1))
            z = jnp.concatenate(z, axis=0)
            spectrum = right_dot(z, forward)
            k = wave[...]
            inverse_k = 1.0 / jnp.maximum(k, 1.0)
            weighted = []
            for j in range(batch):
                cut = prm[turn, j : j + 1]
                damp = prm[turn, UNIT + j : UNIT + j + 1]
                ratio = cut * inverse_k
                factor = jnp.where(k > cut, damp * ratio * ratio, 1.0)
                weighted.append(
                    spectrum[j * kept : (j + 1) * kept] * jnp.concatenate([factor, factor], axis=1)
                )
            weighted = jnp.concatenate(weighted, axis=0)
            v = right_dot(weighted, backward)
            u = []
            for j in range(batch):
                vr = v[j * kept : (j + 1) * kept, :LANES]
                vi = v[j * kept : (j + 1) * kept, LANES:]
                u.append(jnp.concatenate([vr * tr + vi * ti, vi * tr - vr * ti], axis=0))
            u = jnp.concatenate(u, axis=1)
            out = left_dot(last, u)
            for j in range(batch):
                piece = out[:, j * LANES : (j + 1) * LANES] + means[j]
                done[pl.ds((base + j) * depth, depth), :] = piece

        some_rows()

        def circle(m, start):
            t, lane = divmod(start, LANES)

            def tile(t):
                index = lax.rem(m * near_tiles + t + outer, outer)
                return done[pl.ds(index, UNIT, stride=depth), :]

            if lane == 0:
                return tile(t)
            return jnp.concatenate([tile(t)[:, lane:], tile(t + 1)[:, :lane]], axis=1)

        def gather_period(m, carry):
            column = lax.broadcasted_iota(jnp.int32, (UNIT, LANES), 1)
            for source in range(near_sectors):
                target = m * near_sectors + source
                start = source * width
                for lane in range(0, padded, LANES):
                    tile = circle(m, start + lane)
                    if lane + LANES == padded:
                        tile = jnp.where(column < LANES - LEV, tile, circle(m, start - LANES))
                    ret[slot, target, :, lane : lane + LANES] = tile
            return carry

        lax.fori_loop(0, lon_size // near_sectors, gather_period, 0)
        return_copies(slot, push)

    for load in table_loads:
        load.wait()

    if lent_jobs:

        @pl.when(jnp.logical_not(is_polar))
        def _():
            param_copy().wait_recv()
            relayed(0)

    kept_count, lent_count = len(kept_jobs), len(lent_jobs)
    for slot in range(max(kept_count, lent_count)):

        @pl.when(is_polar)
        def _():
            if slot + 1 < kept_count:
                own_copies(slot, sent)
                own_copies(slot + 1, push)
            if slot >= 2 and slot < lent_count:
                for copy in relay_copies(slot - 2):
                    copy.wait_send()
                for copy in relay_copies(slot):
                    copy.start()
            if slot == 0 and lent_count > 1:
                for copy in relay_copies(1):
                    copy.start()

        if slot + 1 < lent_count:

            @pl.when(jnp.logical_not(is_polar))
            def _():
                relayed(slot + 1)

        if slot < kept_count and slot < lent_count:
            work(slot)
        elif slot < kept_count:
            pl.when(is_polar)(functools.partial(work, slot))
        else:
            pl.when(jnp.logical_not(is_polar))(functools.partial(work, slot))

    @pl.when(is_polar)
    def _():
        if lent_jobs:
            param_copy().wait_send()
            for slot in range(max(0, lent_count - 2), lent_count):
                for copy in relay_copies(slot):
                    copy.wait_send()
        own_copies(kept_count - 1, sent)
        for slot in range(kept_count):
            return_copies(slot, sent)
        for plane, jobs in enumerate((kept_jobs, lent_jobs)):
            for slot, (fields, turn) in enumerate(jobs):
                for source in range(lon_size):
                    group = turn * span + source % span
                    field = fields[source // span]
                    arrived(filt.at[1 + group, field], ret_recv.at[slot, plane, source])

    if lent_jobs:

        @pl.when(jnp.logical_not(is_polar))
        def _():
            for slot in range(lent_count):
                spread_copies(slot, sent)
                return_copies(slot, sent)

    @pl.when(jnp.logical_not(is_polar))
    def _():
        keep_copy().wait()
        for side in range(2):
            for item in range(3):
                rim_copy(side, item).wait_send()

    for side, rim in enumerate((0, groups + 1)):
        at_pole = band == (0 if side == 0 else lat_size - 1)
        arrived(filt.at[rim, 2], halo_recv.at[side, 1])

        @pl.when(jnp.logical_not(at_pole))
        def _():
            arrived(filt.at[rim, 1], halo_recv.at[side, 0])
            arrived(filt.at[rim, 3], halo_recv.at[side, 2])


def stencil_kernel(steps, lat_size, ratio, where_ref, below, *rest):
    parts = SUB // UNIT
    here, above, coef, uv, new_h, new_q = rest[:parts], *rest[parts:]
    step = pl.program_id(0)
    band = where_ref[0]
    width = new_h.shape[-1]
    padded = below.shape[-1]
    low_pole = (step == 0) & (band == 0)
    high_pole = (step == steps - 1) & (band == lat_size - 1)
    u, v, h, q = [jnp.concatenate([part[0, f] for part in here], axis=0) for f in range(4)]

    def south_of(x, f):
        row = below[0, f, UNIT - 1 : UNIT, :]
        pole = below[0, f, 0:1, :] if f == 2 else jnp.zeros_like(row)
        return jnp.concatenate([jnp.where(low_pole, pole, row), x[: SUB - 1]], axis=0)

    def north_of(x, f):
        row = above[0, f, 0:1, :]
        pole = above[0, f, UNIT - 1 : UNIT, :] if f == 2 else jnp.zeros_like(row)
        return jnp.concatenate([x[1:], jnp.where(high_pole, pole, row)], axis=0)

    def east_of(x):
        return pltpu.roll(x, padded - LEV, 1)

    def west_of(x):
        return pltpu.roll(x, LEV, 1)

    inv_c = coef[:, 0:1]
    face_s = coef[:, 1:2]
    face_n = coef[:, 2:3]
    he, hs, hn = east_of(h), south_of(h, 2), north_of(h, 2)
    hw = west_of(h)
    wind = 0.25 * (u + east_of(u))
    fx = wind * (h + he)
    gx = wind * (q + east_of(q))
    wind_s = face_s * (south_of(v, 1) + v)
    wind_n = face_n * (v + north_of(v, 1))
    fy = wind_n * (h + hn) - wind_s * (hs + h)
    gy = wind_n * (q + north_of(q, 3)) - wind_s * (south_of(q, 3) + q)
    out_h = h - ((fx - west_of(fx)) + fy) * inv_c
    out_q = q - ((gx - west_of(gx)) + gy) * inv_c
    out_u = u - (he - hw) * (0.5 * inv_c)
    out_v = v - (hn - hs) * (0.5 * ratio)
    uv[0] = out_u[:, :width]
    uv[1] = out_v[:, :width]
    new_h[...] = out_h[:, :width]
    new_q[...] = out_q[:, :width]


def per_device(winds, thickness, tracer, cutoff, damping):
    lat_size = lax.axis_size("lat")
    lon_size = lax.axis_size("lon")
    band = lax.axis_index("lat")
    row_count, width = thickness.shape
    columns = width // LEV
    length = columns * lon_size
    nlat = row_count * lat_size
    inner = LANES // LEV
    depth = round_up(length // inner, 2 * SUB)
    padded = round_up(width + 2 * LEV, LANES)
    groups, turns, span, split, kept_jobs, lent_jobs = plan(lat_size, lon_size, row_count)
    slots = max(len(kept_jobs), len(lent_jobs))
    relays = max(1, len(lent_jobs))
    tables = [jnp.asarray(t) for t in dft_tables(length, inner)]
    vmem_spec = pl.BlockSpec(memory_space=pltpu.VMEM)
    hbm_spec = pl.BlockSpec(memory_space=pltpu.HBM)
    smem_spec = pl.BlockSpec(memory_space=pltpu.SMEM)
    f32 = jnp.float32
    filt = pl.pallas_call(
        functools.partial(filter_kernel, lat_size, lon_size),
        out_shape=jax.ShapeDtypeStruct((groups + 2, 4, UNIT, padded), f32),
        in_specs=[hbm_spec] * 3 + [smem_spec] * 2 + [hbm_spec] * TABLES,
        out_specs=vmem_spec,
        scratch_shapes=[pltpu.VMEM(t.shape, t.dtype) for t in tables]
        + [
            pltpu.VMEM((relays, split, span, UNIT, padded), f32),
            pltpu.VMEM((slots, lon_size, UNIT, padded), f32),
            pltpu.VMEM((UNIT * depth, LANES), f32),
            pltpu.VMEM((UNIT * depth, LANES), f32),
            pltpu.VMEM((slots, lon_size, UNIT, padded), f32),
            pltpu.VMEM((4, row_count, width), f32),
            pltpu.VMEM((groups + 2, 4, UNIT, padded), f32),
            pltpu.VMEM((3, groups, UNIT, LANES), f32),
            pltpu.VMEM((2, 3, groups, UNIT, LANES), f32),
            pltpu.VMEM((turns, 2 * UNIT, LANES), f32),
            pltpu.SemaphoreType.DMA((relays, split)),
            pltpu.SemaphoreType.DMA((relays, split)),
            pltpu.SemaphoreType.DMA((slots, lon_size)),
            pltpu.SemaphoreType.DMA((slots, lon_size)),
            pltpu.SemaphoreType.DMA((slots, lon_size)),
            pltpu.SemaphoreType.DMA((slots, 2, lon_size)),
            pltpu.SemaphoreType.DMA((slots, 2, lon_size)),
            pltpu.SemaphoreType.DMA((2, 3)),
            pltpu.SemaphoreType.DMA((2, 3)),
            pltpu.SemaphoreType.DMA((4,)),
            pltpu.SemaphoreType.DMA((2,)),
            pltpu.SemaphoreType.DMA((2,)),
            pltpu.SemaphoreType.DMA((2,)),
            pltpu.SemaphoreType.DMA((1,)),
            pltpu.SemaphoreType.DMA((TABLES,)),
        ],
        compiler_params=pltpu.CompilerParams(
            collective_id=0, has_side_effects=True, vmem_limit_bytes=54 * 1024 * 1024
        ),
        cost_estimate=pl.CostEstimate(
            flops=4 * 10**9, bytes_accessed=4 * row_count * padded * 8, transcendentals=0
        ),
        name="polar_filter",
    )(winds, thickness, tracer, cutoff, damping, *tables)

    dlam = 2.0 * math.pi / length
    dphi = math.pi / nlat
    ratio = dlam / dphi
    centers = np.cos(-np.pi / 2 + (np.arange(nlat) + 0.5) * dphi)
    faces = np.cos(-np.pi / 2 + np.arange(nlat + 1) * dphi)
    faces[0] = faces[-1] = 0.0
    faces = 0.25 * ratio * faces
    coef = jnp.asarray(np.stack([1.0 / centers, faces[:-1], faces[1:]], axis=1), f32)
    steps = row_count // SUB
    where_am_i = band.astype(jnp.int32).reshape(1)
    block = (1, 4, UNIT, padded)

    def block_of(part, i, b):
        return (i * (SUB // UNIT) + part, 0, 0, 0)

    uv, new_h, new_q = pl.pallas_call(
        functools.partial(stencil_kernel, steps, lat_size, ratio),
        grid_spec=pltpu.PrefetchScalarGridSpec(
            num_scalar_prefetch=1,
            grid=(steps,),
            in_specs=[
                pl.BlockSpec(block, functools.partial(block_of, part))
                for part in range(SUB // UNIT + 2)
            ]
            + [
                pl.BlockSpec((SUB, 3), lambda i, b: (b[0] * steps + i, 0)),
            ],
            out_specs=(
                pl.BlockSpec((2, SUB, width), lambda i, b: (0, i, 0)),
                pl.BlockSpec((SUB, width), lambda i, b: (i, 0)),
                pl.BlockSpec((SUB, width), lambda i, b: (i, 0)),
            ),
        ),
        out_shape=(
            jax.ShapeDtypeStruct((2, row_count, width), f32),
            jax.ShapeDtypeStruct((row_count, width), f32),
            jax.ShapeDtypeStruct((row_count, width), f32),
        ),
        compiler_params=pltpu.CompilerParams(vmem_limit_bytes=20 * 1024 * 1024),
        name="stencil",
    )(where_am_i, *[filt] * (SUB // UNIT + 2), coef)
    return uv, new_h, new_q


def solution(mesh):
    placed = (P(None, "lat", "lon"), P("lat", "lon"), P("lat", "lon"), P("lat"), P("lat"))
    return jax.shard_map(
        per_device,
        mesh=mesh,
        in_specs=placed,
        out_specs=(P(None, "lat", "lon"), P("lat", "lon"), P("lat", "lon")),
        check_vma=False,
    )
```

```python
import functools
import math

import jax
import jax.numpy as jnp
import numpy as np
from jax import lax
from jax.experimental import pallas as pl
from jax.experimental.pallas import tpu as pltpu
from jax.sharding import PartitionSpec as P

LEV = 8
LANES = 128
SUB = 8
UNIT = 4
MESH = pl.DeviceIdType.MESH
TABLES = 7


def round_up(value, step):
    return -(-value // step) * step


def halves(x):
    high = x.astype(jnp.bfloat16)
    return high, (x - high.astype(jnp.float32)).astype(jnp.bfloat16)


def left_dot(parts, x):
    high, low = halves(x)
    stacked = jnp.concatenate([high, low, high], axis=0)
    return jnp.dot(parts[...], stacked, preferred_element_type=jnp.float32)


def right_dot(x, parts):
    high, low = halves(x)
    stacked = jnp.concatenate([high, low, high], axis=1)
    return jnp.dot(stacked, parts[...], preferred_element_type=jnp.float32)


def dft_tables(length, inner):
    outer = length // inner
    depth = round_up(outer, 2 * SUB)
    half = outer // 2 + 1
    kept = round_up(half, SUB)
    p = np.arange(outer)
    k1 = np.arange(half)
    angle = 2.0 * np.pi * ((p[None, :] * k1[:, None]) % outer) / outer
    first = np.zeros((2 * kept, depth))
    first[:half, :outer] = np.cos(angle)
    first[kept : kept + half, :outer] = -np.sin(angle)
    twice = np.where((k1 == 0) | (2 * k1 == outer), 1.0, 2.0)[:, None] / length
    last = np.zeros((depth, 2 * kept))
    last[:outer, :half] = (twice * np.cos(angle)).T
    last[:outer, kept : kept + half] = (-twice * np.sin(angle)).T
    a = np.arange(inner)
    turn = 2.0 * np.pi * ((k1[:, None] * a[None, :]) % length) / length
    twiddle = np.zeros((2, kept, LANES))
    twiddle[0, :half, : inner * LEV] = np.repeat(np.cos(turn), LEV, axis=1)
    twiddle[1, :half, : inner * LEV] = np.repeat(-np.sin(turn), LEV, axis=1)
    small = 2.0 * np.pi * ((a[:, None] * a[None, :]) % inner) / inner
    eye = np.eye(LEV)

    def real_form(re, im):
        out = np.zeros((2 * LANES, 2 * LANES))
        used = inner * LEV
        out[:used, :used] = np.kron(re, eye)
        out[:used, LANES : LANES + used] = np.kron(im, eye)
        out[LANES : LANES + used, :used] = -np.kron(im, eye)
        out[LANES : LANES + used, LANES : LANES + used] = np.kron(re, eye)
        return out

    forward = real_form(np.cos(small), -np.sin(small))
    backward = real_form(np.cos(small), np.sin(small))
    k = k1[:, None] + outer * a[None, :]
    wave = np.zeros((kept, LANES))
    wave[:half, : inner * LEV] = np.repeat(np.minimum(k, length - k), LEV, axis=1)
    average = np.zeros((LANES, LANES))
    average[: inner * LEV, : inner * LEV] = np.kron(np.ones((inner, inner)), eye) / length

    def left_parts(table):
        high, low = halves(np.asarray(table, np.float32))
        return np.concatenate([high, high, low], axis=1)

    def right_parts(table):
        high, low = halves(np.asarray(table, np.float32))
        return np.concatenate([high, high, low], axis=0)

    matrices = [left_parts(first), right_parts(forward), right_parts(backward), left_parts(last)]
    return matrices + [np.asarray(t, np.float32) for t in (twiddle, wave, average)]


def plan(lat_size, lon_size, row_count):
    groups = row_count // UNIT
    turns = max(1, groups // lon_size)
    span = groups // turns
    split = lon_size // span
    jobs = []
    for field in range(0, 4, split):
        jobs += [(tuple(range(field, field + split)), turn) for turn in range(turns)]
    lent = len(jobs) // 2
    return groups, turns, span, split, jobs[: len(jobs) - lent], jobs[len(jobs) - lent :]


def filter_kernel(
    lat_size,
    lon_size,
    winds,
    thickness,
    tracer,
    cutoff,
    damping,
    *rest,
):
    table_in, rest = rest[:TABLES], rest[TABLES:]
    filt, rest = rest[0], rest[1:]
    tables, rest = rest[:TABLES], rest[TABLES:]
    first, forward, backward, last, twiddle, wave, average = tables
    (

        relay,
    recv,
    spread,
    done,
    ret,
    own,
    ext,
    edge,
    edge_in,
    prm,
    relay_send,
    relay_recv,
    fwd_send,
    fwd_recv,
    ret_send,
    ret_recv,
    halo_send,
    halo_recv,
    rim_send,
    own_sem,
    edge_send,
    edge_recv,
    prm_sem,
    filt_sem,
    table_sem,
    ) = rest
    row_count, width = thickness.shape
    padded = filt.shape[-1]
    groups, turns, span, split, kept_jobs, lent_jobs = plan(lat_size, lon_size, row_count)
    planes = 2 if lent_jobs else 1
    outer = width * lon_size // LANES
    depth = first.shape[1] // 3
    period = math.lcm(width, LANES)
    near_sectors, near_tiles = period // width, period // LANES
    kept = wave.shape[0]
    quarter = lat_size // 4
    bit = 1 << (lat_size.bit_length() - 3)
    polar_bands = [b for b in range(lat_size) if b < quarter or b >= lat_size - quarter]
    band = lax.axis_index("lat")
    lon = lax.axis_index("lon")
    is_polar = (band < quarter) | (band >= lat_size - quarter)
    lowbit = (band // bit) % 2
    partner = band + bit - 2 * bit * lowbit
    home = jnp.where(is_polar, band, partner)
    my_plane = jnp.where(is_polar, 0, 1)
    my_place = lax.rem(lon, span)
    my_split = lon // span

    def pair_of(b):
        return {b, b ^ bit} if planes == 2 else {b}

    linked = [[False] * lat_size for _ in range(lat_size)]
    for b in range(lat_size):
        linked[b][b] = True
    for pb in polar_bands:
        for worker in pair_of(pb):
            targets = pair_of(pb) | {t for t in (pb - 1, pb + 1) if 0 <= t < lat_size}
            for target in targets:
                linked[worker][target] = linked[target][worker] = True

    table_loads = [
        pltpu.make_async_copy(table_in[i], tables[i], table_sem.at[i]) for i in range(TABLES)
    ]
    arrays = [winds.at[0], winds.at[1], thickness, tracer]
    loads = [pltpu.make_async_copy(arrays[f], own.at[f], own_sem.at[f]) for f in range(4)]
    for load in loads + table_loads:
        load.start()
    barrier = pltpu.get_barrier_semaphore()
    expected = jnp.int32(-1)
    for other in range(lat_size):
        who = [b for b in range(lat_size) if linked[b][other]]
        talks = functools.reduce(jnp.logical_or, [band == b for b in who])
        expected += jnp.where(talks, lon_size, 0)

        @pl.when(talks)
        def _():
            for step in range(lon_size):
                target = lax.rem(lon + step, lon_size)

                @pl.when((target != lon) | (band != other))
                def _():
                    pl.semaphore_signal(
                        barrier, inc=1, device_id={"lat": other, "lon": target}, device_id_type=MESH
                    )

        near = [b for b in range(lat_size) if abs(b - other) == 1 and not linked[b][other]]
        if near:
            beside = functools.reduce(jnp.logical_or, [band == b for b in near])
            expected += jnp.where(beside, 1, 0)

            @pl.when(beside)
            def _():
                pl.semaphore_signal(
                    barrier, inc=1, device_id={"lat": other, "lon": lon}, device_id_type=MESH
                )

    pl.semaphore_wait(barrier, expected)

    def copies(src, dst, ssem, rsem, lat_to, lon_to):
        remote = pltpu.make_async_remote_copy(
            src_ref=src,
            dst_ref=dst,
            send_sem=ssem,
            recv_sem=rsem,
            device_id={"lat": lat_to, "lon": lon_to},
            device_id_type=MESH,
        )
        local = pltpu.make_async_copy(src, dst, rsem)
        return remote, local

    def push(src, dst, ssem, rsem, lat_to, lon_to):
        remote, local = copies(src, dst, ssem, rsem, lat_to, lon_to)
        same = (lat_to == band) & (lon_to == lon)

        @pl.when(same)
        def _():
            local.start()

        @pl.when(jnp.logical_not(same))
        def _():
            remote.start()

    def sent(src, dst, ssem, rsem, lat_to, lon_to):
        remote, _ = copies(src, dst, ssem, rsem, lat_to, lon_to)
        same = (lat_to == band) & (lon_to == lon)

        @pl.when(jnp.logical_not(same))
        def _():
            remote.wait_send()

    def arrived(dst, rsem):
        pltpu.make_async_copy(dst, dst, rsem).wait()

    def own_copies(slot, action):
        fields, turn = kept_jobs[slot]
        for step in range(span):
            place = lax.rem(lon + step, span)
            for part in range(split):
                target = part * span + place
                action(
                    ext.at[1 + turn * span + place, fields[part]],
                    recv.at[slot, lon],
                    fwd_send.at[slot, target],
                    fwd_recv.at[slot, lon],
                    band,
                    target,
                )

    def relay_copies(slot):
        fields, turn = lent_jobs[slot]
        return [
            pltpu.make_async_remote_copy(
                src_ref=ext.at[pl.ds(1 + turn * span, span), fields[part]],
                dst_ref=relay.at[slot, part],
                send_sem=relay_send.at[slot, part],
                recv_sem=relay_recv.at[slot, part],
                device_id={"lat": partner, "lon": lon},
                device_id_type=MESH,
            )
            for part in range(split)
        ]

    def spread_copies(slot, action):
        for step in range(span):
            place = lax.rem(lon + step, span)
            for part in range(split):
                target = part * span + place
                action(
                    relay.at[slot, part, place],
                    recv.at[slot, lon],
                    fwd_send.at[slot, target],
                    fwd_recv.at[slot, lon],
                    band,
                    target,
                )

    def relayed(slot):
        for copy in relay_copies(slot):
            copy.wait_recv()
        spread_copies(slot, push)

    def stage(field, turn):
        def one(i, carry):
            tile = turn * (span * UNIT // SUB) + i
            rows = own[field, pl.ds(pl.multiple_of(tile * SUB, SUB), SUB), :]
            for part in range(SUB // UNIT):
                block = rows[part * UNIT : (part + 1) * UNIT]
                ext[1 + tile * (SUB // UNIT) + part, field, :, :width] = block
            return carry

        lax.fori_loop(0, span * UNIT // SUB, one, 0)

    def stage_job(job):
        for field in job[0]:
            stage(field, job[1])

    spread[...] = jnp.zeros_like(spread)
    for load in loads:
        load.wait()

    def param_copy():
        return pltpu.make_async_remote_copy(
            src_ref=prm,
            dst_ref=prm,
            send_sem=prm_sem.at[0],
            recv_sem=prm_sem.at[1],
            device_id={"lat": partner, "lon": lon},
            device_id_type=MESH,
        )

    @pl.when(is_polar)
    def _():
        for job in lent_jobs[:1]:
            stage_job(job)
            for copy in relay_copies(0):
                copy.start()
        stage_job(kept_jobs[0])
        own_copies(0, push)
        for turn in range(turns):
            for j in range(UNIT):
                row = (turn * span + my_place) * UNIT + j
                low, high = j, UNIT + j
                prm[turn, low : low + 1] = jnp.full((1, LANES), cutoff[row].astype(jnp.float32))
                prm[turn, high : high + 1] = jnp.full((1, LANES), damping[row])
        for job in kept_jobs[1:] + lent_jobs[1:]:
            stage_job(job)
        if planes == 2:
            param_copy().start()

    def edge_copy(side):
        shift = 1 if side else lon_size - 1
        return pltpu.make_async_remote_copy(
            src_ref=edge,
            dst_ref=edge_in.at[side],
            send_sem=edge_send.at[side],
            recv_sem=edge_recv.at[side],
            device_id={"lat": band, "lon": lax.rem(lon + shift, lon_size)},
            device_id_type=MESH,
        )

    def rim_copy(side, item):
        return pltpu.make_async_remote_copy(
            src_ref=ext.at[1 if side == 0 else groups, item + 1],
            dst_ref=filt.at[groups + 1 if side == 0 else 0, item + 1],
            send_sem=rim_send.at[side, item],
            recv_sem=halo_recv.at[1 - side, item],
            device_id={"lat": band - 1 if side == 0 else band + 1, "lon": lon},
            device_id_type=MESH,
        )

    def keep_copy():
        inner_groups = pl.ds(1, groups)
        return pltpu.make_async_copy(ext.at[inner_groups], filt.at[inner_groups], filt_sem.at[0])

    @pl.when(jnp.logical_not(is_polar))
    def _():
        for field in range(4):
            for turn in range(turns):
                stage(field, turn)
        for item, f in enumerate((0, 2, 3)):
            edge[item, :, :, :LEV] = ext[1 : groups + 1, f, :, :LEV]
            edge[item, :, :, LEV : 2 * LEV] = ext[1 : groups + 1, f, :, width - LEV : width]
        edge_copy(0).start()
        edge_copy(1).start()
        edge_copy(0).wait()
        edge_copy(1).wait()
        for item, f in enumerate((0, 2, 3)):
            ext[1 : groups + 1, f, :, width : width + LEV] = edge_in[0, item, :, :, :LEV]
            ext[1 : groups + 1, f, :, padded - LEV :] = edge_in[1, item, :, :, LEV : 2 * LEV]
        keep_copy().start()
        for side in range(2):
            for item in range(3):
                rim_copy(side, item).start()

    def job_of(slot):
        def pick(jobs):
            fields, turn = jobs[min(slot, len(jobs) - 1)]
            field = jnp.int32(fields[0])
            for part in range(1, split):
                field = jnp.where(my_split == part, fields[part], field)
            return field, jnp.int32(turn)

        field, turn = pick(kept_jobs)
        if lent_jobs:
            lent_field, lent_turn = pick(lent_jobs)
            field = jnp.where(is_polar, field, lent_field)
            turn = jnp.where(is_polar, turn, lent_turn)
        return field, turn

    def return_copies(slot, action):
        field, turn = job_of(slot)
        group = turn * span + my_place
        for step in range(lon_size):
            target = lax.rem(lon + step, lon_size)
            action(
                ret.at[slot, target],
                filt.at[1 + group, field],
                ret_send.at[slot, target],
                ret_recv.at[slot, my_plane, lon],
                home,
                target,
            )
        item = jnp.maximum(field - 1, 0)
        opposite = lon_size // 2
        for side in range(2):
            at_edge = group == (0 if side == 0 else groups - 1)
            at_pole = home == (0 if side == 0 else lat_size - 1)
            lat_to = home - 1 if side == 0 else home + 1

            @pl.when(at_edge & (field >= 1) & jnp.logical_not(at_pole))
            def _():
                for target in range(lon_size):
                    action(
                        ret.at[slot, target],
                        filt.at[groups + 1 if side == 0 else 0, item + 1],
                        halo_send.at[slot, side, target],
                        halo_recv.at[1 - side, item],
                        lat_to,
                        jnp.int32(target),
                    )

            @pl.when(at_edge & (field == 2) & at_pole)
            def _():
                for target in range(lon_size):
                    action(
                        ret.at[slot, target],
                        filt.at[0 if side == 0 else groups + 1, 2],
                        halo_send.at[slot, side, target],
                        halo_recv.at[side, 1],
                        home,
                        jnp.int32((target + opposite) % lon_size),
                    )

    batch = UNIT

    def work(slot):
        _, turn = job_of(slot)
        for s in range(lon_size):
            arrived(recv.at[slot, s], fwd_recv.at[slot, s])

        def spread_period(m, carry):
            for t in range(near_tiles):
                source, lane = divmod(t * LANES, width)
                take = min(LANES, width - lane)
                tile = recv[slot, m * near_sectors + source, :, lane : lane + take]
                if take < LANES:
                    more = recv[slot, m * near_sectors + source + 1, :, : LANES - take]
                    tile = jnp.concatenate([tile, more], axis=1)
                spread[pl.ds(m * near_tiles + t, UNIT, stride=depth), :] = tile
            return carry

        lax.fori_loop(0, lon_size // near_sectors, spread_period, 0)

        def some_rows():
            base = 0
            rows = [spread[pl.ds((base + j) * depth, depth), :] for j in range(batch)]
            sums = [jnp.sum(row, axis=0, keepdims=True) for row in rows] * (SUB // batch)
            mean = jnp.dot(
                jnp.concatenate(sums, axis=0),
                average[...],
                preferred_element_type=jnp.float32,
            )
            means = [mean[j : j + 1] for j in range(batch)]
            x = jnp.concatenate([rows[j] - means[j] for j in range(batch)], axis=1)
            y = left_dot(first, x)
            tr, ti = twiddle[0], twiddle[1]
            z = []
            for j in range(batch):
                yr = y[:kept, j * LANES : (j + 1) * LANES]
                yi = y[kept:, j * LANES : (j + 1) * LANES]
                z.append(jnp.concatenate([yr * tr - yi * ti, yr * ti + yi * tr], axis=1))
            z = jnp.concatenate(z, axis=0)
            spectrum = right_dot(z, forward)
            k = wave[...]
            inverse_k = 1.0 / jnp.maximum(k, 1.0)
            weighted = []
            for j in range(batch):
                cut = prm[turn, j : j + 1]
                damp = prm[turn, UNIT + j : UNIT + j + 1]
                ratio = cut * inverse_k
                factor = jnp.where(k > cut, damp * ratio * ratio, 1.0)
                weighted.append(
                    spectrum[j * kept : (j + 1) * kept] * jnp.concatenate([factor, factor], axis=1)
                )
            weighted = jnp.concatenate(weighted, axis=0)
            v = right_dot(weighted, backward)
            u = []
            for j in range(batch):
                vr = v[j * kept : (j + 1) * kept, :LANES]
                vi = v[j * kept : (j + 1) * kept, LANES:]
                u.append(jnp.concatenate([vr * tr + vi * ti, vi * tr - vr * ti], axis=0))
            u = jnp.concatenate(u, axis=1)
            out = left_dot(last, u)
            for j in range(batch):
                piece = out[:, j * LANES : (j + 1) * LANES] + means[j]
                done[pl.ds((base + j) * depth, depth), :] = piece

        some_rows()

        def circle(m, start):
            t, lane = divmod(start, LANES)

            def tile(t):
                index = lax.rem(m * near_tiles + t + outer, outer)
                return done[pl.ds(index, UNIT, stride=depth), :]

            if lane == 0:
                return tile(t)
            return jnp.concatenate([tile(t)[:, lane:], tile(t + 1)[:, :lane]], axis=1)

        def gather_period(m, carry):
            column = lax.broadcasted_iota(jnp.int32, (UNIT, LANES), 1)
            for source in range(near_sectors):
                target = m * near_sectors + source
                start = source * width
                for lane in range(0, padded, LANES):
                    tile = circle(m, start + lane)
                    if lane + LANES == padded:
                        tile = jnp.where(column < LANES - LEV, tile, circle(m, start - LANES))
                    ret[slot, target, :, lane : lane + LANES] = tile
            return carry

        lax.fori_loop(0, lon_size // near_sectors, gather_period, 0)
        return_copies(slot, push)

    for load in table_loads:
        load.wait()

    if lent_jobs:

        @pl.when(jnp.logical_not(is_polar))
        def _():
            param_copy().wait_recv()
            relayed(0)

    kept_count, lent_count = len(kept_jobs), len(lent_jobs)
    for slot in range(max(kept_count, lent_count)):

        @pl.when(is_polar)
        def _():
            if slot + 1 < kept_count:
                own_copies(slot, sent)
                own_copies(slot + 1, push)
            if slot >= 1 and slot + 1 < lent_count:
                for copy in relay_copies(slot - 1):
                    copy.wait_send()
                for copy in relay_copies(slot + 1):
                    copy.start()
            if slot == 0 and lent_count > 1:
                for copy in relay_copies(1):
                    copy.start()

        if slot + 1 < lent_count:

            @pl.when(jnp.logical_not(is_polar))
            def _():
                relayed(slot + 1)

        if slot < kept_count and slot < lent_count:
            work(slot)
        elif slot < kept_count:
            pl.when(is_polar)(functools.partial(work, slot))
        else:
            pl.when(jnp.logical_not(is_polar))(functools.partial(work, slot))

    @pl.when(is_polar)
    def _():
        if lent_jobs:
            param_copy().wait_send()
            for slot in range(max(0, lent_count - 2), lent_count):
                for copy in relay_copies(slot):
                    copy.wait_send()
        own_copies(kept_count - 1, sent)
        for slot in range(kept_count):
            return_copies(slot, sent)
        for plane, jobs in enumerate((kept_jobs, lent_jobs)):
            for slot, (fields, turn) in enumerate(jobs):
                for source in range(lon_size):
                    group = turn * span + source % span
                    field = fields[source // span]
                    arrived(filt.at[1 + group, field], ret_recv.at[slot, plane, source])

    if lent_jobs:

        @pl.when(jnp.logical_not(is_polar))
        def _():
            for slot in range(lent_count):
                spread_copies(slot, sent)
                return_copies(slot, sent)

    @pl.when(jnp.logical_not(is_polar))
    def _():
        keep_copy().wait()
        for side in range(2):
            for item in range(3):
                rim_copy(side, item).wait_send()

    for side, rim in enumerate((0, groups + 1)):
        at_pole = band == (0 if side == 0 else lat_size - 1)
        arrived(filt.at[rim, 2], halo_recv.at[side, 1])

        @pl.when(jnp.logical_not(at_pole))
        def _():
            arrived(filt.at[rim, 1], halo_recv.at[side, 0])
            arrived(filt.at[rim, 3], halo_recv.at[side, 2])


def stencil_kernel(steps, lat_size, ratio, where_ref, below, *rest):
    parts = SUB // UNIT
    here, above, coef, uv, new_h, new_q = rest[:parts], *rest[parts:]
    step = pl.program_id(0)
    band = where_ref[0]
    width = new_h.shape[-1]
    padded = below.shape[-1]
    low_pole = (step == 0) & (band == 0)
    high_pole = (step == steps - 1) & (band == lat_size - 1)
    u, v, h, q = [jnp.concatenate([part[0, f] for part in here], axis=0) for f in range(4)]

    def south_of(x, f):
        row = below[0, f, UNIT - 1 : UNIT, :]
        pole = below[0, f, 0:1, :] if f == 2 else jnp.zeros_like(row)
        return jnp.concatenate([jnp.where(low_pole, pole, row), x[: SUB - 1]], axis=0)

    def north_of(x, f):
        row = above[0, f, 0:1, :]
        pole = above[0, f, UNIT - 1 : UNIT, :] if f == 2 else jnp.zeros_like(row)
        return jnp.concatenate([x[1:], jnp.where(high_pole, pole, row)], axis=0)

    def east_of(x):
        return pltpu.roll(x, padded - LEV, 1)

    def west_of(x):
        return pltpu.roll(x, LEV, 1)

    inv_c = coef[:, 0:1]
    face_s = coef[:, 1:2]
    face_n = coef[:, 2:3]
    he, hs, hn = east_of(h), south_of(h, 2), north_of(h, 2)
    hw = west_of(h)
    wind = 0.25 * (u + east_of(u))
    fx = wind * (h + he)
    gx = wind * (q + east_of(q))
    wind_s = face_s * (south_of(v, 1) + v)
    wind_n = face_n * (v + north_of(v, 1))
    fy = wind_n * (h + hn) - wind_s * (hs + h)
    gy = wind_n * (q + north_of(q, 3)) - wind_s * (south_of(q, 3) + q)
    out_h = h - ((fx - west_of(fx)) + fy) * inv_c
    out_q = q - ((gx - west_of(gx)) + gy) * inv_c
    out_u = u - (he - hw) * (0.5 * inv_c)
    out_v = v - (hn - hs) * (0.5 * ratio)
    uv[0] = out_u[:, :width]
    uv[1] = out_v[:, :width]
    new_h[...] = out_h[:, :width]
    new_q[...] = out_q[:, :width]


def per_device(winds, thickness, tracer, cutoff, damping):
    lat_size = lax.axis_size("lat")
    lon_size = lax.axis_size("lon")
    band = lax.axis_index("lat")
    row_count, width = thickness.shape
    columns = width // LEV
    length = columns * lon_size
    nlat = row_count * lat_size
    inner = LANES // LEV
    depth = round_up(length // inner, 2 * SUB)
    padded = round_up(width + 2 * LEV, LANES)
    groups, turns, span, split, kept_jobs, lent_jobs = plan(lat_size, lon_size, row_count)
    slots = max(len(kept_jobs), len(lent_jobs))
    relays = max(1, len(lent_jobs))
    tables = [jnp.asarray(t) for t in dft_tables(length, inner)]
    vmem_spec = pl.BlockSpec(memory_space=pltpu.VMEM)
    hbm_spec = pl.BlockSpec(memory_space=pltpu.HBM)
    smem_spec = pl.BlockSpec(memory_space=pltpu.SMEM)
    f32 = jnp.float32
    filt = pl.pallas_call(
        functools.partial(filter_kernel, lat_size, lon_size),
        out_shape=jax.ShapeDtypeStruct((groups + 2, 4, UNIT, padded), f32),
        in_specs=[hbm_spec] * 3 + [smem_spec] * 2 + [hbm_spec] * TABLES,
        out_specs=vmem_spec,
        scratch_shapes=[pltpu.VMEM(t.shape, t.dtype) for t in tables]
        + [
            pltpu.VMEM((relays, split, span, UNIT, padded), f32),
            pltpu.VMEM((slots, lon_size, UNIT, padded), f32),
            pltpu.VMEM((UNIT * depth, LANES), f32),
            pltpu.VMEM((UNIT * depth, LANES), f32),
            pltpu.VMEM((slots, lon_size, UNIT, padded), f32),
            pltpu.VMEM((4, row_count, width), f32),
            pltpu.VMEM((groups + 2, 4, UNIT, padded), f32),
            pltpu.VMEM((3, groups, UNIT, LANES), f32),
            pltpu.VMEM((2, 3, groups, UNIT, LANES), f32),
            pltpu.VMEM((turns, 2 * UNIT, LANES), f32),
            pltpu.SemaphoreType.DMA((relays, split)),
            pltpu.SemaphoreType.DMA((relays, split)),
            pltpu.SemaphoreType.DMA((slots, lon_size)),
            pltpu.SemaphoreType.DMA((slots, lon_size)),
            pltpu.SemaphoreType.DMA((slots, lon_size)),
            pltpu.SemaphoreType.DMA((slots, 2, lon_size)),
            pltpu.SemaphoreType.DMA((slots, 2, lon_size)),
            pltpu.SemaphoreType.DMA((2, 3)),
            pltpu.SemaphoreType.DMA((2, 3)),
            pltpu.SemaphoreType.DMA((4,)),
            pltpu.SemaphoreType.DMA((2,)),
            pltpu.SemaphoreType.DMA((2,)),
            pltpu.SemaphoreType.DMA((2,)),
            pltpu.SemaphoreType.DMA((1,)),
            pltpu.SemaphoreType.DMA((TABLES,)),
        ],
        compiler_params=pltpu.CompilerParams(
            collective_id=0, has_side_effects=True, vmem_limit_bytes=54 * 1024 * 1024
        ),
        cost_estimate=pl.CostEstimate(
            flops=4 * 10**9, bytes_accessed=4 * row_count * padded * 8, transcendentals=0
        ),
        name="polar_filter",
    )(winds, thickness, tracer, cutoff, damping, *tables)

    dlam = 2.0 * math.pi / length
    dphi = math.pi / nlat
    ratio = dlam / dphi
    centers = np.cos(-np.pi / 2 + (np.arange(nlat) + 0.5) * dphi)
    faces = np.cos(-np.pi / 2 + np.arange(nlat + 1) * dphi)
    faces[0] = faces[-1] = 0.0
    faces = 0.25 * ratio * faces
    coef = jnp.asarray(np.stack([1.0 / centers, faces[:-1], faces[1:]], axis=1), f32)
    steps = row_count // SUB
    where_am_i = band.astype(jnp.int32).reshape(1)
    block = (1, 4, UNIT, padded)

    def block_of(part, i, b):
        return (i * (SUB // UNIT) + part, 0, 0, 0)

    uv, new_h, new_q = pl.pallas_call(
        functools.partial(stencil_kernel, steps, lat_size, ratio),
        grid_spec=pltpu.PrefetchScalarGridSpec(
            num_scalar_prefetch=1,
            grid=(steps,),
            in_specs=[
                pl.BlockSpec(block, functools.partial(block_of, part))
                for part in range(SUB // UNIT + 2)
            ]
            + [
                pl.BlockSpec((SUB, 3), lambda i, b: (b[0] * steps + i, 0)),
            ],
            out_specs=(
                pl.BlockSpec((2, SUB, width), lambda i, b: (0, i, 0)),
                pl.BlockSpec((SUB, width), lambda i, b: (i, 0)),
                pl.BlockSpec((SUB, width), lambda i, b: (i, 0)),
            ),
        ),
        out_shape=(
            jax.ShapeDtypeStruct((2, row_count, width), f32),
            jax.ShapeDtypeStruct((row_count, width), f32),
            jax.ShapeDtypeStruct((row_count, width), f32),
        ),
        compiler_params=pltpu.CompilerParams(vmem_limit_bytes=20 * 1024 * 1024),
        name="stencil",
    )(where_am_i, *[filt] * (SUB // UNIT + 2), coef)
    return uv, new_h, new_q


def solution(mesh):
    placed = (P(None, "lat", "lon"), P("lat", "lon"), P("lat", "lon"), P("lat"), P("lat"))
    return jax.shard_map(
        per_device,
        mesh=mesh,
        in_specs=placed,
        out_specs=(P(None, "lat", "lon"), P("lat", "lon"), P("lat", "lon")),
        check_vma=False,
    )
```
